256 devices in a mesh: wa: 16 (over x, z_hi, core), tu: 4 (over y), tv: 4 (over z_lo).
Axes of the slice: x: 4, y: 4, z: 8 (z_hi: 2, z_lo: 4; z = z_hi * 4 + z_lo), core: 2. Of those that a mesh axis runs over, the one named last changes fastest.
Arguments:
- kernel_u: bfloat16 [4096, 256, 128], P(('wa', 'tu', 'tv')), may hold values from -0.5 to 0.5
- kernel_v: bfloat16 [4096, 256, 128], P(('wa', 'tu', 'tv')), may hold values from -0.5 to 0.5
- visibilities: bfloat16 [4096, 2, 256], P(('wa', 'tu', 'tv')), may hold values from -6 to 6
- vis_count: int32 [4096], P(('wa', 'tu', 'tv')), may hold values from 1 to 256
- tile_route: int32 [4096, 1], P(('wa', 'tu', 'tv')), may hold values from 0 to 15; in each aligned block of 16 rows (0 to 15, 16 to 31, ...) at most 2 rows name the same one
- block_offset: int32 [4096, 2], P(('wa', 'tu', 'tv')), may hold values from 0 to 896
- plane_w: float32 [16], P('wa'), may hold values from -300 to 300
Outputs:
- image: float32 [4096, 4096], P('wa', ('tu', 'tv'))
The draws below stay inside these ranges and needn't reach their ends.
Inputs may be any that keep to these rules, and one draw needn't show every extreme that they name: `tile_route`: of the 16 blocks entering one device (aligned blocks of rows), at most 2 go to the same uv tile, and exactly 2 go to one tile from some device. `block_offset`: A block's subgrid lies inside its tile.
All inputs are finite; a program needn't handle non-finite values.
Results may differ from the reference program's by a relative error of at most 0.025.
Values may be sent and summed in bfloat16 or wider, within the bound.
No kernel may reach another device: no remote copies, remote signals or barrier semaphores. Data moves between devices by JAX's collectives and lax.ppermute only.
A program may use at most 64 MiB of HBM per device.

```python
import math
import jax
import jax.numpy as jnp
import numpy as np
from jax import lax

N = 8192
P_SIZE = 64
C = 256
S = 128
BLK_DEV = 16
TILE_U = 1024
TILE_V = 1024
PLANES = 16
BLOCKS = 4096
CAP = 2
N_TU = 4
N_TV = 4


def with_ends(drawn, own_key, least, largest):
    spot = [jax.random.randint(jax.random.fold_in(own_key, axis), (), 0, length) for axis, length in enumerate(drawn.shape)]
    longest = drawn.shape.index(max(drawn.shape))
    beside = spot[:longest] + [(spot[longest] + 1) % drawn.shape[longest]] + spot[longest + 1:]
    return drawn.at[tuple(spot)].set(least).at[tuple(beside)].set(largest)


def levels(key, dims, pieces, low, largest):
    loudness, own = 1.0, jax.random.fold_in(key, 6)
    for dim, shards_of in pieces:
        heights = jnp.exp(jax.random.uniform(jax.random.fold_in(own, dim), (shards_of,), jnp.float32, low / len(pieces), largest / len(pieces)))
        loudness = loudness * jnp.repeat(heights, dims[dim] // shards_of).reshape([-1 if axis == dim else 1 for axis in range(len(dims))])
    return loudness


def shared_out(own_key, own, number, rows, count, top, reach, slope):
    order = jax.random.permutation(own_key, count)
    heavy_load, ordinary = shares(count, rows * top, reach, slope, True), shares(count, rows * top, reach, slope, False)
    places = jnp.arange(count)

    def named(tallies, turn):
        used = int((tallies > 0).sum())
        fixed = max(1, used // 4)
        passed = fixed + (places - fixed + turn * (used - fixed)) % max(1, count - fixed)
        return jnp.zeros((count,), jnp.int32).at[order[jnp.where(places < fixed, places, passed)]].set(jnp.asarray(tallies, jnp.int32))

    tallies = jnp.where(number % 4 == 0, named(heavy_load, number // 4), named(ordinary, number - number // 4 - 1))
    mixed = jax.random.permutation(jax.random.fold_in(own, 3), count)
    giver, receiver = mixed[0:count // 2 * 2:2], mixed[1:count // 2 * 2:2]
    room = jnp.minimum(tallies[giver] - 1, reach - tallies[receiver]) // 2
    room = jnp.where((giver == order[0]) | (receiver == order[0]) | (tallies[receiver] == 0), 0, jnp.maximum(room, 0))
    passed = jax.random.randint(jax.random.fold_in(own, 4), (count // 2,), 0, 1 << 20) % (room + 1)
    tallies = tallies.at[giver].add(-passed).at[receiver].add(passed)
    items = jnp.searchsorted(jnp.cumsum(tallies), jnp.arange(rows * top), side="right").astype(jnp.int32)
    table = items.reshape(top, rows).T
    table = table[jax.random.permutation(jax.random.fold_in(own, 1), rows)]
    turn = jax.random.randint(jax.random.fold_in(own, 2), (rows, 1), 0, top)
    return jnp.take_along_axis(table, (jnp.arange(top)[None, :] + turn) % top, axis=1)


def shares(count, total, limit, lean, full):
    portions = [(1 << 20) // math.isqrt(grade ** lean) + 1 for grade in range(1, count + 1)]
    largest = limit if full else min(limit, max(-(-total // count), total * portions[0] // sum(portions)))
    least = 1 if total - largest >= count - 1 else 0
    given, spare = [largest] + [least] * (count - 1), total - largest - least * (count - 1)
    while spare > 0:
        free = [i for i in range(1, count) if given[i] < largest] or [i for i in range(1, count) if given[i] < limit]
        whole, budget = sum([portions[i] for i in free]), spare
        for i in free:
            more = min(limit - given[i], max(1, budget * portions[i] // whole), spare)
            given[i] = given[i] + more
            spare = spare - more
    return np.array(given)


def centred(rng, dims, deviation, most, split=(), kind=jnp.bfloat16):
    values = deviation * jax.random.normal(rng, dims, jnp.float32)
    if split:
        values = values * levels(rng, dims, split, -0.22, 0.18)
    return jnp.clip(values, -most, most).astype(kind)


def setup_inputs(seed: int = 0) -> dict:
    streams_of = jax.random.split(jax.random.key(seed), 8)
    kernel_u = centred(streams_of[0], (BLOCKS, C, S), S ** -0.5, 0.5, ((0, 256),))
    kernel_v = centred(streams_of[1], (BLOCKS, C, S), S ** -0.5, 0.5, ((0, 256),))
    visibilities = centred(streams_of[2], (BLOCKS, 2, C), 1.0, 6.0, ((0, 256),))
    vis_count = with_ends(jax.random.randint(streams_of[3], (BLOCKS,), 1, C + 1), jax.random.fold_in(streams_of[3], 1), 1, C).astype(jnp.int32)
    tile_route_keys = jax.random.split(jax.random.fold_in(streams_of[4], 1), BLOCKS // BLK_DEV)
    tile_route_turns = jax.random.permutation(jax.random.fold_in(streams_of[4], 3), BLOCKS // BLK_DEV)
    tile_route = jax.vmap(lambda own, number: shared_out(jax.random.fold_in(streams_of[4], 2), own, number, BLK_DEV, N_TU * N_TV, 1, CAP, 2))(tile_route_keys, tile_route_turns).reshape((BLOCKS, 1))
    block_offset = with_ends(jax.random.randint(streams_of[5], (BLOCKS, 2), 0, min(TILE_U, TILE_V) - S + 1), jax.random.fold_in(streams_of[5], 1), 0, min(TILE_U, TILE_V) - S).astype(jnp.int32)
    plane_w = jnp.clip(jax.random.uniform(streams_of[6], (PLANES,), jnp.float32, -300.0, 300.0) * levels(streams_of[6], (PLANES,), ((0, 16),), -0.4, 0.0), -300.0, 300.0)
    return dict(kernel_u=kernel_u, kernel_v=kernel_v, visibilities=visibilities, vis_count=vis_count, tile_route=tile_route, block_offset=block_offset, plane_w=plane_w)


field_half = 0.25

def first_table(q_len, r_len):
    q_idx = jnp.arange(q_len, dtype=jnp.int32)
    c_idx = jnp.arange(r_len, dtype=jnp.int32)
    angles = (q_idx[:, None] * c_idx[None, :] % r_len).astype(jnp.float32) * (2.0 * math.pi / r_len)
    cosine = jnp.cos(angles)
    sine_part = jnp.sin(angles)
    real_in = jnp.stack([cosine, sine_part], axis=1)
    imag_in = jnp.stack([-sine_part, cosine], axis=1)
    return jnp.stack([real_in, imag_in], axis=0).astype(jnp.bfloat16)

def twiddle_parts(p_len, r_len):
    p_idx = jnp.arange(p_len, dtype=jnp.int32)
    c_idx = jnp.arange(r_len, dtype=jnp.int32)
    angles = (p_idx[:, None] * c_idx[None, :]).astype(jnp.float32) * (2.0 * math.pi / N)
    return (jnp.cos(angles), jnp.sin(angles))

def last_table(p_len, e_vals):
    p_idx = jnp.arange(p_len, dtype=jnp.int32)
    angles = (p_idx[:, None] * e_vals[None, :] % p_len).astype(jnp.float32) * (2.0 * math.pi / p_len)
    cosine = jnp.cos(angles)
    sine_part = jnp.sin(angles)
    real_in = jnp.stack([cosine, sine_part], axis=2)
    imag_in = jnp.stack([-sine_part, cosine], axis=2)
    return jnp.stack([real_in, imag_in], axis=1).astype(jnp.bfloat16)

def rotate(values, cos_t, sin_t, axis):
    real_part = lax.index_in_dim(values, 0, axis, keepdims=False).astype(jnp.float32)
    imag_part = lax.index_in_dim(values, 1, axis, keepdims=False).astype(jnp.float32)
    rotated = jnp.stack([real_part * cos_t - imag_part * sin_t, real_part * sin_t + imag_part * cos_t], axis=axis)
    return rotated.astype(jnp.bfloat16)

def screen_parts(row_ids, col_ids, w_value):
    half_n = N // 2
    cell_size = 2.0 * field_half / N
    dir_l = ((row_ids + half_n) % N - half_n).astype(jnp.float32) * cell_size
    dir_m = ((col_ids + half_n) % N - half_n).astype(jnp.float32) * cell_size
    n_lift = jnp.sqrt(1.0 - dir_l[:, None] ** 2 - dir_m[None, :] ** 2) - 1.0
    quarter = ((row_ids[:, None] + col_ids[None, :]) % 4).astype(jnp.float32)
    angles = 2.0 * math.pi * w_value * n_lift - 0.5 * math.pi * quarter
    return (jnp.cos(angles), jnp.sin(angles))

def block_subgrid(vis_block, live_count, ku_block, kv_block):
    live_mask = jnp.arange(C, dtype=jnp.int32) < live_count
    masked = jnp.where(live_mask[None, :], vis_block, jnp.zeros_like(vis_block)).astype(jnp.float32)
    weighted = (masked[:, :, None] * ku_block.astype(jnp.float32)[None, :, :]).astype(jnp.bfloat16)
    sub_grid = jnp.einsum('xcs,ct->xst', weighted.astype(jnp.float32), kv_block.astype(jnp.float32))
    return sub_grid.astype(jnp.bfloat16)

def reference(kernel_u, kernel_v, visibilities, vis_count, tile_route, block_offset, plane_w):
    half_n = N // 2
    per_plane = BLOCKS // PLANES
    tile_count = N_TU * N_TV
    q_len = half_n // P_SIZE
    r_len = N // P_SIZE
    e_loc = P_SIZE // 2 // tile_count
    col_width = e_loc * r_len
    table_one = first_table(q_len, r_len).astype(jnp.float32)
    tw_cos, tw_sin = twiddle_parts(P_SIZE, r_len)
    table_two = last_table(P_SIZE, jnp.arange(P_SIZE // 2, dtype=jnp.int32)).astype(jnp.float32)
    norm_scale = 1.0 / math.sqrt(C * BLOCKS)

    def grid_step(uv_grid, block_item):
        ku_block, kv_block, vis_block, live_count, route_row, offset_row = block_item
        sub_grid = block_subgrid(vis_block, live_count, ku_block, kv_block)
        target = route_row[0]
        row_at = (target // N_TV * TILE_U + offset_row[0]).astype(jnp.int32)
        col_at = (target % N_TV * TILE_V + offset_row[1]).astype(jnp.int32)
        zero_idx = jnp.zeros((), jnp.int32)
        current = lax.dynamic_slice(uv_grid, (zero_idx, row_at, col_at), (2, S, S))
        updated = lax.dynamic_update_slice(uv_grid, current + sub_grid.astype(jnp.float32), (zero_idx, row_at, col_at))
        return (updated, None)

    def plane_step(image_sum, plane_item):
        ku_plane, kv_plane, vis_plane, count_plane, route_plane, offset_plane, w_value = plane_item
        start_grid = jnp.zeros((2, half_n, half_n), jnp.float32)
        uv_grid, _ = lax.scan(grid_step, start_grid, (ku_plane, kv_plane, vis_plane, count_plane, route_plane, offset_plane))
        grid_bf = uv_grid.astype(jnp.bfloat16)
        spread = grid_bf.reshape(2, half_n, q_len, P_SIZE).astype(jnp.float32)
        first_pass = jnp.einsum('xuqp,xqyc->upyc', spread, table_one).astype(jnp.bfloat16)
        turned = rotate(first_pass, tw_cos, tw_sin, 2)
        spectrum = jnp.einsum('upyc,pyez->uezc', turned.astype(jnp.float32), table_two).astype(jnp.bfloat16)
        pencils = jnp.moveaxis(spectrum.reshape(half_n, tile_count, e_loc, 2, r_len), 1, 0)

        def column_term(column_item):
            pencil, block_idx = column_item
            stacked = pencil.reshape(q_len, P_SIZE, e_loc, 2, r_len).astype(jnp.float32)
            second_pass = jnp.einsum('qpexc,xqyd->pdeyc', stacked, table_one).astype(jnp.bfloat16)
            turned_two = rotate(second_pass, tw_cos[:, :, None, None], tw_sin[:, :, None, None], 3)
            planar = jnp.einsum('pdeyc,pyfz->fdezc', turned_two.astype(jnp.float32), table_two)
            flat_rows = planar.reshape(half_n, e_loc, 2, r_len)
            row_ids = jnp.arange(half_n, dtype=jnp.int32)
            col_ids = block_idx * col_width + jnp.arange(col_width, dtype=jnp.int32)
            s_re, s_im = screen_parts(row_ids, col_ids, w_value)
            x_re = flat_rows[:, :, 0, :].reshape(half_n, col_width)
            x_im = flat_rows[:, :, 1, :].reshape(half_n, col_width)
            return ((x_re * s_re - x_im * s_im) * norm_scale).astype(jnp.bfloat16)
        terms = lax.map(column_term, (pencils, jnp.arange(tile_count, dtype=jnp.int32)))
        partial_image = jnp.moveaxis(terms, 0, 1).reshape(half_n, half_n)
        return (image_sum + partial_image.astype(jnp.float32), None)
    plane_items = (kernel_u.reshape(PLANES, per_plane, C, S), kernel_v.reshape(PLANES, per_plane, C, S), visibilities.reshape(PLANES, per_plane, 2, C), vis_count.reshape(PLANES, per_plane), tile_route.reshape(PLANES, per_plane, 1), block_offset.reshape(PLANES, per_plane, 2), plane_w)
    image, _ = lax.scan(plane_step, jnp.zeros((half_n, half_n), jnp.float32), plane_items)
    return image
```

```python
import functools
import math

import jax
import jax.numpy as jnp
import ml_dtypes
import numpy as np
from jax import lax
from jax.experimental import pallas as pl
from jax.experimental.pallas import tpu as pltpu
from jax.sharding import PartitionSpec as P

N = 8192
HALF = 4096
S = 128
RANK = 8
COLS = 256
U0 = 64
U1 = 64
D_LEN = 128
F_LEN = 32
TILE = 1024
CHUNKS = 2
FIELD = 0.25
MIB = 1 << 20


def factor_tables(owners):
    t = np.arange(S) - (S - 1) / 2
    mu = np.arange(COLS) - (COLS - 1) / 2
    angle = 2.0 * np.pi * np.outer(t, mu) / N
    left, right = [], []
    for part in (np.cos(angle), np.sin(angle)):
        u, sv, vh = np.linalg.svd(part, full_matrices=False)
        left.append(u[:, :RANK])
        right.append(sv[:RANK, None] * vh[:RANK])
    basis = np.concatenate(left, axis=1)
    rows = []
    for j in range(owners):
        centre = COLS * j + (COLS - 1) / 2
        turn = np.exp(2j * np.pi * np.arange(S) * centre / N)
        proj = (basis * turn[:, None]).T
        rows.append(np.concatenate([proj.real, -proj.imag], axis=1))
        rows.append(np.concatenate([proj.imag, proj.real], axis=1))
    project = np.concatenate(rows, axis=0).astype(ml_dtypes.bfloat16)
    even, odd = right
    expand = np.concatenate(
        [
            np.concatenate([even, even], axis=1),
            np.concatenate([-odd, odd], axis=1),
            np.concatenate([-even, even], axis=1),
            np.concatenate([-odd, -odd], axis=1),
        ],
        axis=0,
    ).astype(np.float32)
    return project, expand


def row_tables():
    u0 = np.arange(U0)[:, None, None]
    u1 = np.arange(U1)[None, None, :]
    d = np.arange(D_LEN)[None, :, None]
    a = 2.0 * np.pi * (((u0 + U0 * u1) * d) % N) / N
    c, s = np.cos(a), np.sin(a)
    first = np.concatenate(
        [np.concatenate([c, -s], axis=2), np.concatenate([s, c], axis=2)], axis=1
    )
    b = 2.0 * np.pi * ((np.arange(F_LEN)[:, None] * np.arange(U0)[None, :]) % U0) / U0
    c, s = np.cos(b), np.sin(b)
    last = np.concatenate([np.concatenate([c, -s], axis=1), np.concatenate([s, c], axis=1)], axis=0)
    return first.astype(ml_dtypes.bfloat16), last.astype(ml_dtypes.bfloat16)


def project_kernel(count_ref, ku_ref, kv_ref, vis_ref, table_ref, out_ref, *, first_block):
    b = pl.program_id(0)
    live = count_ref[first_block + b]
    slots = lax.broadcasted_iota(jnp.int32, (2, ku_ref.shape[1]), 1)
    vis = jnp.where(slots < live, vis_ref[0].astype(jnp.float32), 0.0)
    kv_t = kv_ref[0].astype(jnp.float32).T
    weighted = jnp.concatenate([kv_t * vis[0:1, :], kv_t * vis[1:2, :]], axis=0)
    sub = jnp.dot(
        weighted.astype(jnp.bfloat16), ku_ref[0], preferred_element_type=jnp.float32
    ).astype(jnp.bfloat16)
    out = jnp.dot(table_ref[...], sub, preferred_element_type=jnp.float32)
    out_ref[...] = out.astype(jnp.bfloat16).reshape(out_ref.shape)


def project_chunk(count, ku, kv, vis, table, owners, chunk, size):
    slots = ku.shape[1]
    first = chunk * size
    return pl.pallas_call(
        functools.partial(project_kernel, first_block=first),
        out_shape=jax.ShapeDtypeStruct((owners, 4 * RANK, size * S), jnp.bfloat16),
        grid_spec=pltpu.PrefetchScalarGridSpec(
            num_scalar_prefetch=1,
            grid=(size,),
            in_specs=[
                pl.BlockSpec((1, slots, S), lambda b, _: (first + b, 0, 0)),
                pl.BlockSpec((1, slots, S), lambda b, _: (first + b, 0, 0)),
                pl.BlockSpec((1, 2, slots), lambda b, _: (first + b, 0, 0)),
                pl.BlockSpec(table.shape, lambda b, _: (0, 0)),
            ],
            out_specs=pl.BlockSpec((owners, 4 * RANK, S), lambda b, _: (0, 0, b)),
        ),
        compiler_params=pltpu.CompilerParams(vmem_limit_bytes=32 * MIB),
        cost_estimate=pl.CostEstimate(
            flops=size * 2 * (256 * 256 * 128 + 512 * 256 * 128),
            bytes_accessed=size * 4 * 65536,
            transcendentals=0,
        ),
    )(count, ku, kv, vis, table)


def add_blocks(row_ref, got_ref, phase_ref, expand_ref, acc_ref, chunk, size, per_src):
    table = expand_ref[...]
    r = RANK

    def per_source(src, carry):
        for b in range(size):
            g = src * per_src + chunk * size + b
            row = row_ref[g]
            ph = phase_ref[pl.ds(g, 1), :]
            swapped = jnp.concatenate([ph[:, COLS:], ph[:, :COLS]], axis=1)
            weights = jnp.concatenate(
                [
                    table[0:r] * ph,
                    table[r : 2 * r] * swapped,
                    table[2 * r : 3 * r] * swapped,
                    table[3 * r : 4 * r] * ph,
                ],
                axis=0,
            ).astype(jnp.bfloat16)
            coeffs = got_ref[src, :, b * S : (b + 1) * S]
            rows = lax.dot_general(
                coeffs, weights, (((0,), (0,)), ((), ())), preferred_element_type=jnp.float32
            )
            for c in range(4):
                acc_ref[c, pl.ds(row, S), :] += rows[:, c * 128 : (c + 1) * 128]
        return carry

    lax.fori_loop(0, got_ref.shape[0], per_source, 0)


def grid_kernel(row_ref, got_ref, phase_ref, expand_ref, *rest, chunk, size, per_src):
    if chunk == 0:
        (out_ref,) = rest
        out_ref[...] = jnp.zeros_like(out_ref)
    else:
        old_ref, out_ref, sem = rest
        copy = pltpu.make_async_copy(old_ref, out_ref, sem)
        copy.start()
        copy.wait()
    add_blocks(row_ref, got_ref, phase_ref, expand_ref, out_ref, chunk, size, per_src)


def grid_chunk(rows, got, phase, expand, old, chunk, size, per_src):
    vmem = pl.BlockSpec(memory_space=pltpu.VMEM)
    operands = [rows, got, phase, expand]
    specs = [pl.BlockSpec(memory_space=pltpu.SMEM), vmem, vmem, vmem]
    scratch = []
    if chunk:
        operands.append(old)
        specs.append(pl.BlockSpec(memory_space=pl.ANY))
        scratch.append(pltpu.SemaphoreType.DMA)
    return pl.pallas_call(
        functools.partial(grid_kernel, chunk=chunk, size=size, per_src=per_src),
        out_shape=jax.ShapeDtypeStruct((4, HALF, 128), jnp.float32),
        in_specs=specs,
        out_specs=vmem,
        scratch_shapes=scratch,
        compiler_params=pltpu.CompilerParams(vmem_limit_bytes=32 * MIB),
        cost_estimate=pl.CostEstimate(
            flops=got.shape[0] * size * 2 * 128 * 256 * 512,
            bytes_accessed=12 * MIB,
            transcendentals=0,
        ),
    )(*operands)


def image_kernel(
    row_ref, place_ref, got_ref, phase_ref, expand_ref, old_ref, first_hbm, last_ref, screen_hbm,
    keep_ref, send_ref, acc_ref, first_ref, mid_ref, screen_ref, full_ref, sems,
    *, chunk, size, per_src,
):
    load_old = pltpu.make_async_copy(old_ref, acc_ref, sems.at[0])
    load_first = pltpu.make_async_copy(first_hbm, first_ref, sems.at[1])
    load_screen = pltpu.make_async_copy(screen_hbm, screen_ref, sems.at[2])
    load_old.start()
    load_first.start()
    load_screen.start()
    load_old.wait()
    add_blocks(row_ref, got_ref, phase_ref, expand_ref, acc_ref, chunk, size, per_src)
    load_first.wait()

    def first_step(u0, carry):
        parts = [acc_ref[c, pl.ds(u0, U1, stride=U0), :] for c in range(4)]
        x = jnp.concatenate(
            [
                jnp.concatenate([parts[0], parts[1]], axis=1),
                jnp.concatenate([parts[2], parts[3]], axis=1),
            ],
            axis=0,
        ).astype(jnp.bfloat16)
        y = jnp.dot(first_ref[u0], x, preferred_element_type=jnp.float32)
        base = pl.multiple_of(u0 * (2 * D_LEN), 2 * D_LEN)
        mid_ref[0, pl.ds(base, 2 * D_LEN), :] = y[:, :128]
        mid_ref[1, pl.ds(base, 2 * D_LEN), :] = y[:, 128:]
        return carry

    lax.fori_loop(0, U0, first_step, 0, unroll=2)
    load_screen.wait()
    last = last_ref[...]

    def last_step(d, carry):
        parts = [
            [mid_ref[c, pl.ds(x * D_LEN + d, U0, stride=2 * D_LEN), :] for c in range(2)]
            for x in range(2)
        ]
        y = jnp.concatenate([jnp.concatenate(p, axis=1) for p in parts], axis=0)
        planar = jnp.dot(last, y.astype(jnp.bfloat16), preferred_element_type=jnp.float32)
        value = planar[:F_LEN] * screen_ref[0, d] - planar[F_LEN:] * screen_ref[1, d]
        for c in range(2):
            full_ref[c, pl.ds(d, F_LEN, stride=D_LEN), :] = value[:, c * 128 : (c + 1) * 128]
        return carry

    lax.fori_loop(0, D_LEN, last_step, 0, unroll=2)
    for out_ref, which in ((keep_ref, 0), (send_ref, 1)):
        for i in range(out_ref.shape[0]):
            base = pl.multiple_of(place_ref[which, i] * COLS, COLS)
            for c in range(2):
                out_ref[i, :, c * 128 : (c + 1) * 128] = full_ref[
                    c, pl.ds(base, COLS), :
                ].astype(jnp.bfloat16)


def make_image(rows, place, got, phase, expand, old, first, last, screen, chunk, size, per_src):
    vmem = pl.BlockSpec(memory_space=pltpu.VMEM)
    smem = pl.BlockSpec(memory_space=pltpu.SMEM)
    hbm = pl.BlockSpec(memory_space=pl.ANY)
    piece = jax.ShapeDtypeStruct((place.shape[1], COLS, COLS), jnp.bfloat16)
    return pl.pallas_call(
        functools.partial(image_kernel, chunk=chunk, size=size, per_src=per_src),
        out_shape=(piece, piece),
        in_specs=[smem, smem, vmem, vmem, vmem, hbm, hbm, vmem, hbm],
        out_specs=(vmem, vmem),
        scratch_shapes=[
            pltpu.VMEM((4, HALF, 128), jnp.float32),
            pltpu.VMEM(first.shape, jnp.bfloat16),
            pltpu.VMEM((2, U0 * 2 * D_LEN, 128), jnp.float32),
            pltpu.VMEM(screen.shape, jnp.float32),
            pltpu.VMEM((2, HALF, 128), jnp.float32),
            pltpu.SemaphoreType.DMA((3,)),
        ],
        compiler_params=pltpu.CompilerParams(vmem_limit_bytes=56 * MIB),
        cost_estimate=pl.CostEstimate(
            flops=4 * 1024**3, bytes_accessed=24 * MIB, transcendentals=0
        ),
    )(rows, place, got, phase, expand, old, first, last, screen)


def screen_parts(col_base, w_value, scale):
    d = jnp.arange(D_LEN, dtype=jnp.int32)[:, None, None]
    f = jnp.arange(F_LEN, dtype=jnp.int32)[None, :, None]
    row = f * D_LEN + d
    col = col_base + jnp.arange(COLS, dtype=jnp.int32)[None, None, :]
    half = N // 2
    cell = 2.0 * FIELD / N
    dl = ((row + half) % N - half).astype(jnp.float32) * cell
    dm = ((col + half) % N - half).astype(jnp.float32) * cell
    lift = jnp.sqrt(1.0 - dl**2 - dm**2) - 1.0
    quarter = ((row + col) % 4).astype(jnp.float32)
    angle = 2.0 * math.pi * w_value * lift - 0.5 * math.pi * quarter
    return jnp.stack([jnp.cos(angle), jnp.sin(angle)]) * scale


def sum_planes(keep, send, planes):
    def shifted(values, target):
        pairs = [(i, target(i)) for i in range(planes)]
        return lax.ppermute(values, "wa", pairs).astype(jnp.float32)

    total = keep.astype(jnp.float32) + shifted(send, lambda i: i ^ 1)
    total = total.astype(jnp.bfloat16).reshape(4, 2, COLS, COLS)
    got = [
        shifted(total[step], lambda i, step=step: (i + 4 * step) % planes) for step in (1, 2, 3)
    ]
    total = (total[0].astype(jnp.float32) + got[0] + got[1] + got[2]).astype(jnp.bfloat16)
    return total[0].astype(jnp.float32) + shifted(total[1], lambda i: i ^ 2)


def body(kernel_u, kernel_v, visibilities, vis_count, tile_route, block_offset, plane_w):
    n_tu, n_tv, planes = lax.axis_size("tu"), lax.axis_size("tv"), lax.axis_size("wa")
    owners = n_tu * n_tv
    blocks, slots = kernel_u.shape[0], kernel_u.shape[1]
    size = blocks // CHUNKS
    project, expand = factor_tables(owners)
    first, last = row_tables()

    target = tile_route[:, 0]
    corner = jnp.stack(
        [target // n_tv * TILE + block_offset[:, 0], target % n_tv * TILE + block_offset[:, 1]],
        axis=0,
    )
    corners = lax.all_gather(corner, ("tu", "tv"), axis=0)
    rows = corners[:, 0, :].reshape(-1)
    cols = corners[:, 1, :].reshape(-1)

    owner = lax.axis_index(("tu", "tv"))
    col_base = owner * COLS
    lane = jnp.arange(COLS, dtype=jnp.int32)
    turns = (cols[:, None] * (col_base + lane)[None, :]) % N
    shift = (S - 1) / 2 * (lane.astype(jnp.float32) - (COLS - 1) / 2)
    angle = (turns.astype(jnp.float32) + shift[None, :]) * (2.0 * math.pi / N)
    phase = jnp.concatenate([jnp.cos(angle), jnp.sin(angle)], axis=1)

    scale = 1.0 / math.sqrt(slots * blocks * owners * 16)
    screen = screen_parts(col_base, plane_w[0], scale)

    got = []
    for chunk in range(CHUNKS):
        coeffs = project_chunk(
            vis_count, kernel_u, kernel_v, visibilities, project, owners, chunk, size
        )
        got.append(
            lax.all_to_all(coeffs, ("tu", "tv"), split_axis=0, concat_axis=0, tiled=True)
        )
    me = lax.axis_index("wa")
    core, z_hi, x = me % 2, me // 2 % 2, me // 4
    step = jnp.arange(8, dtype=jnp.int32)
    pair = ((x + step // 2) % 4) * 4 + (z_hi ^ (step % 2)) * 2
    place = jnp.stack([pair + core, pair + (1 - core)])

    acc = None
    for chunk in range(CHUNKS - 1):
        acc = grid_chunk(rows, got[chunk], phase, expand, acc, chunk, size, blocks)
    keep, send = make_image(
        rows, place, got[-1], phase, expand, acc, first, last, screen, CHUNKS - 1, size, blocks
    )
    if planes != 16:
        return keep, send
    return sum_planes(keep, send, planes)


def solution(mesh):
    split = ("wa", "tu", "tv")
    placed = (
        P(split, None, None),
        P(split, None, None),
        P(split, None, None),
        P(split),
        P(split, None),
        P(split, None),
        P("wa"),
    )
    return jax.shard_map(
        body, mesh=mesh, in_specs=placed, out_specs=P("wa", ("tu", "tv")), check_vma=False
    )
```

```python
import functools
import math

import jax
import jax.numpy as jnp
import ml_dtypes
import numpy as np
from jax import lax
from jax.experimental import pallas as pl
from jax.experimental.pallas import tpu as pltpu
from jax.sharding import PartitionSpec as P

N = 8192
HALF = 4096
S = 128
EVEN, ODD = 8, 7
RANK = 8
MARK = 15
COLS = 256
U0 = 512
U1 = 8
L0 = 16
L1 = 256
TILE = 1024
CHUNKS = 2
STEP = 4
FIELD = 0.25
MIB = 1 << 20


def factor_tables(owners):
    t = np.arange(S) - (S - 1) / 2
    mu = np.arange(COLS) - (COLS - 1) / 2
    angle = 2.0 * np.pi * np.outer(t, mu) / N
    left, right = [], []
    for part, rank in ((np.cos(angle), EVEN), (np.sin(angle), ODD)):
        u, sv, vh = np.linalg.svd(part, full_matrices=False)
        pad = ((0, RANK - rank), (0, 0))
        left.append(np.pad(u[:, :rank].T, pad))
        right.append(np.pad(sv[:rank, None] * vh[:rank], pad))
    basis = np.concatenate(left, axis=0)
    rows = []
    for j in range(owners):
        centre = COLS * j + (COLS - 1) / 2
        turn = np.exp(2j * np.pi * np.arange(S) * centre / N)
        proj = basis * turn[None, :]
        rows.append(np.concatenate([proj.real, -proj.imag], axis=1))
        rows.append(np.concatenate([proj.imag, proj.real], axis=1))
    project = np.concatenate(rows, axis=0).astype(ml_dtypes.bfloat16)
    even, odd = right
    expand = np.concatenate(
        [
            np.concatenate([even, even], axis=1),
            np.concatenate([-odd, odd], axis=1),
            np.concatenate([-even, even], axis=1),
            np.concatenate([-odd, -odd], axis=1),
        ],
        axis=0,
    ).astype(np.float32)
    return project, expand


def row_table():
    u0 = np.arange(U0)[None, None, :]
    l0 = np.arange(L0)[:, None, None]
    l1 = np.arange(L1)[None, :, None]
    a = 2.0 * np.pi * ((u0 * (l0 + L0 * l1)) % N) / N
    c, s = np.cos(a).astype(ml_dtypes.bfloat16), np.sin(a).astype(ml_dtypes.bfloat16)
    table = np.concatenate(
        [np.concatenate([c, -s], axis=2), np.concatenate([s, c], axis=2)], axis=1
    )
    return np.stack([table[0::2], table[1::2]])


def project_kernel(count_ref, ku_ref, kv_ref, vis_ref, table_ref, mark_ref, out_ref, *, first):
    step = pl.program_id(0)
    slots = lax.broadcasted_iota(jnp.int32, (2, ku_ref.shape[1]), 1)
    owners, rows, _ = out_ref.shape
    table = table_ref[...]
    mark = jnp.concatenate([mark_ref[...], mark_ref[...]], axis=1)
    line = lax.broadcasted_iota(jnp.int32, (rows, 2 * S), 0)
    for pair in range(STEP // 2):
        subs = []
        for b in (2 * pair, 2 * pair + 1):
            live = count_ref[first + step * STEP + b]
            vis = jnp.where(slots < live, vis_ref[b].astype(jnp.float32), 0.0)
            kv_t = kv_ref[b].astype(jnp.float32).T
            weighted = jnp.concatenate([kv_t * vis[0:1, :], kv_t * vis[1:2, :]], axis=0)
            subs.append(
                jnp.dot(
                    weighted.astype(jnp.bfloat16), ku_ref[b], preferred_element_type=jnp.float32
                ).astype(jnp.bfloat16)
            )
        out = jnp.dot(
            table, jnp.concatenate(subs, axis=1), preferred_element_type=jnp.float32
        ).reshape(owners, rows, 2 * S)
        out = jnp.where((line == MARK)[None], mark[None], out)
        out_ref[:, :, pair * 2 * S : (pair + 1) * 2 * S] = out.astype(jnp.bfloat16)


def project_chunk(count, ku, kv, vis, table, mark, owners, chunk, size):
    slots = ku.shape[1]
    at = chunk * size // STEP
    return pl.pallas_call(
        functools.partial(project_kernel, first=chunk * size),
        out_shape=jax.ShapeDtypeStruct((owners, 4 * RANK, size * S), jnp.bfloat16),
        grid_spec=pltpu.PrefetchScalarGridSpec(
            num_scalar_prefetch=1,
            grid=(size // STEP,),
            in_specs=[
                pl.BlockSpec((STEP, slots, S), lambda b, _: (at + b, 0, 0)),
                pl.BlockSpec((STEP, slots, S), lambda b, _: (at + b, 0, 0)),
                pl.BlockSpec((STEP, 2, slots), lambda b, _: (at + b, 0, 0)),
                pl.BlockSpec(table.shape, lambda b, _: (0, 0)),
                pl.BlockSpec(mark.shape, lambda b, _: (0, 0)),
            ],
            out_specs=pl.BlockSpec((owners, 4 * RANK, STEP * S), lambda b, _: (0, 0, b)),
        ),
        compiler_params=pltpu.CompilerParams(vmem_limit_bytes=60 * MIB),
        cost_estimate=pl.CostEstimate(
            flops=size * 2 * (256 * 256 * 128 + 512 * 256 * 128),
            bytes_accessed=size * 4 * 65536,
            transcendentals=0,
        ),
    )(count, ku, kv, vis, table, mark)


def add_blocks(row_ref, got_ref, phase_ref, expand_ref, acc_ref, chunk, size, per_src):
    table = expand_ref[...]
    r = RANK

    def per_source(src, carry):
        for b in range(size):
            g = src * per_src + chunk * size + b
            row = row_ref[g]
            ph = phase_ref[pl.ds(g, 1), :]
            swapped = jnp.concatenate([ph[:, COLS:], ph[:, :COLS]], axis=1)
            weights = jnp.concatenate(
                [
                    table[0:r] * ph,
                    table[r : 2 * r] * swapped,
                    table[2 * r : 3 * r] * swapped,
                    table[3 * r : 4 * r] * ph,
                ],
                axis=0,
            ).astype(jnp.bfloat16)
            coeffs = got_ref[src, :, b * S : (b + 1) * S]
            rows = lax.dot_general(
                coeffs, weights, (((0,), (0,)), ((), ())), preferred_element_type=jnp.float32
            )
            for c in range(4):
                acc_ref[c, pl.ds(row, S), :] += rows[:, c * 128 : (c + 1) * 128]
        return carry

    lax.fori_loop(0, got_ref.shape[0], per_source, 0)


def grid_kernel(row_ref, got_ref, phase_ref, expand_ref, out_ref, *, chunk, size, per_src):
    out_ref[...] = jnp.zeros_like(out_ref)
    add_blocks(row_ref, got_ref, phase_ref, expand_ref, out_ref, chunk, size, per_src)


def grid_chunk(rows, got, phase, expand, chunk, size, per_src):
    vmem = pl.BlockSpec(memory_space=pltpu.VMEM)
    return pl.pallas_call(
        functools.partial(grid_kernel, chunk=chunk, size=size, per_src=per_src),
        out_shape=jax.ShapeDtypeStruct((4, HALF, 128), jnp.float32),
        in_specs=[pl.BlockSpec(memory_space=pltpu.SMEM), vmem, vmem, vmem],
        out_specs=vmem,
        compiler_params=pltpu.CompilerParams(vmem_limit_bytes=56 * MIB),
        cost_estimate=pl.CostEstimate(
            flops=got.shape[0] * size * 2 * 128 * 256 * 512,
            bytes_accessed=12 * MIB,
            transcendentals=0,
        ),
    )(rows, got, phase, expand)


def dft8(x):
    def add(p, q):
        return (p[0] + q[0], p[1] + q[1])

    def sub(p, q):
        return (p[0] - q[0], p[1] - q[1])

    def turn(p):
        return (-p[1], p[0])

    def dft4(a, b, c, d):
        s, t, v, w = add(a, c), sub(a, c), add(b, d), turn(sub(b, d))
        return add(s, v), add(t, w), sub(s, v), sub(t, w)

    h = math.sqrt(0.5)
    e = dft4(x[0], x[2], x[4], x[6])
    o = list(dft4(x[1], x[3], x[5], x[7]))
    o[1] = ((o[1][0] - o[1][1]) * h, (o[1][0] + o[1][1]) * h)
    o[2] = turn(o[2])
    o[3] = ((-o[3][0] - o[3][1]) * h, (o[3][0] - o[3][1]) * h)
    return [add(e[k], o[k]) for k in range(4)] + [sub(e[k], o[k]) for k in range(4)]


def finish(place_ref, table_ref, mid_ref, screen_ref, full_ref, keep_ref, send_ref, ready):
    def last_step(k, carry):
        ready(k)
        planar = jnp.dot(table_ref[k], mid_ref[k], preferred_element_type=jnp.float32)
        value = planar[:L1] * screen_ref[k, 0] - planar[L1:] * screen_ref[k, 1]
        full_ref[:, k] = value.astype(jnp.bfloat16).reshape(L1 // 16, 16, COLS)
        return carry

    lax.fori_loop(0, L0 // 2, last_step, 0)
    for out_ref, which in ((keep_ref, 0), (send_ref, 1)):
        for i in range(out_ref.shape[0]):
            out_ref[i] = full_ref[place_ref[which, i]]


def even_kernel(
    row_ref, place_ref, got_ref, phase_ref, expand_ref, old_hbm, table_hbm, screen_hbm,
    keep_ref, send_ref, odd_ref, acc_ref, old_ref, table_ref, mid_ref, screen_ref, full_ref, sems,
    *, chunk, size, per_src,
):
    load_old = pltpu.make_async_copy(old_hbm, old_ref, sems.at[0])
    load_table = pltpu.make_async_copy(table_hbm.at[0], table_ref, sems.at[1])
    load_screen = pltpu.make_async_copy(screen_hbm.at[pl.ds(0, L0 // 2)], screen_ref, sems.at[2])
    load_old.start()
    load_table.start()
    load_screen.start()
    acc_ref[...] = jnp.zeros_like(acc_ref)
    add_blocks(row_ref, got_ref, phase_ref, expand_ref, acc_ref, chunk, size, per_src)
    load_old.wait()

    def first_step(i, carry):
        at = pl.multiple_of(i * 16, 16)
        for half in range(2):
            x = [
                tuple(
                    acc_ref[2 * p + half, pl.ds(at + U0 * k, 16), :]
                    + old_ref[2 * p + half, pl.ds(at + U0 * k, 16), :]
                    for p in range(2)
                )
                for k in range(U1)
            ]
            even = dft8(x)
            for k in range(1, U1):
                c, s = math.cos(math.pi * k / U1), math.sin(math.pi * k / U1)
                x[k] = (x[k][0] * c - x[k][1] * s, x[k][0] * s + x[k][1] * c)
            for ref, out in ((mid_ref, even), (odd_ref, dft8(x))):
                for k in range(L0 // 2):
                    for p in range(2):
                        ref[k, pl.ds(U0 * p + at, 16), half * 128 : (half + 1) * 128] = out[k][
                            p
                        ].astype(jnp.bfloat16)
        return carry

    lax.fori_loop(0, U0 // 16, first_step, 0)
    load_table.wait()
    load_screen.wait()
    finish(
        place_ref, table_ref, mid_ref, screen_ref, full_ref, keep_ref, send_ref, lambda k: None
    )


def odd_kernel(
    place_ref, mid_ref, table_hbm, screen_hbm,
    keep_ref, send_ref, table_ref, screen_ref, full_ref, sems,
):
    def loads(k):
        return (
            pltpu.make_async_copy(table_hbm.at[1, k], table_ref.at[k], sems.at[0, k]),
            pltpu.make_async_copy(screen_hbm.at[L0 // 2 + k], screen_ref.at[k], sems.at[1, k]),
        )

    for k in range(L0 // 2):
        for load in loads(k):
            load.start()

    def ready(k):
        for load in loads(k):
            load.wait()

    finish(place_ref, table_ref, mid_ref, screen_ref, full_ref, keep_ref, send_ref, ready)


def make_image(rows, place, got, phase, expand, old, table, screen, chunk, size, per_src):
    vmem = pl.BlockSpec(memory_space=pltpu.VMEM)
    smem = pl.BlockSpec(memory_space=pltpu.SMEM)
    hbm = pl.BlockSpec(memory_space=pl.ANY)
    half = L0 // 2
    piece = jax.ShapeDtypeStruct((place.shape[1], half, 16, COLS), jnp.bfloat16)
    mid = (half, 2 * U0, COLS)
    buffers = [
        pltpu.VMEM(table.shape[1:], jnp.bfloat16),
        pltpu.VMEM((half, *screen.shape[1:]), jnp.float32),
        pltpu.VMEM((16, half, 16, COLS), jnp.bfloat16),
    ]
    keep, send, odd = pl.pallas_call(
        functools.partial(even_kernel, chunk=chunk, size=size, per_src=per_src),
        out_shape=(piece, piece, jax.ShapeDtypeStruct(mid, jnp.bfloat16)),
        in_specs=[smem, smem, vmem, vmem, vmem, hbm, hbm, hbm],
        out_specs=(vmem, vmem, vmem),
        scratch_shapes=[
            pltpu.VMEM(old.shape, jnp.float32),
            pltpu.VMEM(old.shape, jnp.float32),
            buffers[0],
            pltpu.VMEM(mid, jnp.bfloat16),
            *buffers[1:],
            pltpu.SemaphoreType.DMA((3,)),
        ],
        compiler_params=pltpu.CompilerParams(vmem_limit_bytes=50 * MIB),
        cost_estimate=pl.CostEstimate(
            flops=16 * 1024**3, bytes_accessed=24 * MIB, transcendentals=0
        ),
    )(rows, place, got, phase, expand, old, table, screen)
    keep_odd, send_odd = pl.pallas_call(
        odd_kernel,
        out_shape=(piece, piece),
        in_specs=[smem, vmem, hbm, hbm],
        out_specs=(vmem, vmem),
        scratch_shapes=[*buffers, pltpu.SemaphoreType.DMA((2, half))],
        compiler_params=pltpu.CompilerParams(vmem_limit_bytes=60 * MIB),
        cost_estimate=pl.CostEstimate(
            flops=4 * 1024**3, bytes_accessed=12 * MIB, transcendentals=0
        ),
    )(place, odd, table, screen)
    return (keep, send), (keep_odd, send_odd)


def screen_kernel(base_ref, w_ref, out_ref, *, scale):
    k = pl.program_id(0)
    l0 = 2 * lax.rem(k, L0 // 2) + k // (L0 // 2)
    row = l0 + L0 * lax.broadcasted_iota(jnp.int32, (L1, COLS), 0)
    col = base_ref[0] + lax.broadcasted_iota(jnp.int32, (L1, COLS), 1)
    cell = 2.0 * FIELD / N
    dl = row.astype(jnp.float32) * cell
    dm = col.astype(jnp.float32) * cell
    lift = jnp.sqrt(1.0 - dl * dl - dm * dm) - 1.0
    quarters = (4.0 * w_ref[0]) * lift
    whole = jnp.floor(quarters + 0.5)
    f = quarters - whole
    count = whole.astype(jnp.int32) - row - col
    t = f * f
    h = math.pi / 2
    sine, cosine = 0.0, 0.0
    for n in (11, 9, 7, 5, 3, 1):
        sine = sine * t + (-1) ** (n // 2) * h**n / math.factorial(n)
    for n in (12, 10, 8, 6, 4, 2, 0):
        cosine = cosine * t + (-1) ** (n // 2) * h**n / math.factorial(n)
    sine = sine * f
    odd = (count & 1) == 1
    c = jnp.where(odd, sine, cosine)
    s = jnp.where(odd, cosine, sine)
    out_ref[0, 0] = jnp.where(((count + 1) & 2) == 2, -scale, scale) * c
    out_ref[0, 1] = jnp.where((count & 2) == 2, -scale, scale) * s


def make_screen(base, w, scale):
    smem = pl.BlockSpec(memory_space=pltpu.SMEM)
    return pl.pallas_call(
        functools.partial(screen_kernel, scale=scale),
        out_shape=jax.ShapeDtypeStruct((L0, 2, L1, COLS), jnp.float32),
        grid=(L0,),
        in_specs=[smem, smem],
        out_specs=pl.BlockSpec((1, 2, L1, COLS), lambda k: (k, 0, 0, 0)),
        compiler_params=pltpu.CompilerParams(vmem_limit_bytes=60 * MIB),
        cost_estimate=pl.CostEstimate(
            flops=40 * HALF * COLS, bytes_accessed=8 * MIB, transcendentals=HALF * COLS
        ),
    )(base, w)


def sum_planes(keep, send, planes):
    def shifted(values, target):
        pairs = [(i, target(i)) for i in range(planes)]
        return lax.ppermute(values, "wa", pairs).astype(jnp.float32)

    total = keep.astype(jnp.float32) + shifted(send, lambda i: i ^ 1)
    total = total.astype(jnp.bfloat16).reshape(4, 2, L0 // 2, 16, COLS)
    got = [
        shifted(total[step], lambda i, step=step: (i + 4 * step) % planes) for step in (1, 2, 3)
    ]
    total = (total[0].astype(jnp.float32) + got[0] + got[1] + got[2]).astype(jnp.bfloat16)
    return total[0].astype(jnp.float32) + shifted(total[1], lambda i: i ^ 2)


def body(kernel_u, kernel_v, visibilities, vis_count, tile_route, block_offset, plane_w):
    n_tu, n_tv, planes = lax.axis_size("tu"), lax.axis_size("tv"), lax.axis_size("wa")
    owners = n_tu * n_tv
    blocks, slots = kernel_u.shape[0], kernel_u.shape[1]
    size = blocks // CHUNKS
    project, expand = factor_tables(owners)
    table = row_table()

    target = tile_route[:, 0]
    corner = jnp.stack(
        [target // n_tv * TILE + block_offset[:, 0], target % n_tv * TILE + block_offset[:, 1]],
        axis=0,
    )
    halves = jnp.stack([corner // 64, corner % 64], axis=1).reshape(1, 4 * blocks)
    mark = jnp.pad(halves, ((0, 0), (0, S - 4 * blocks))).astype(jnp.float32)
    owner = lax.axis_index(("tu", "tv"))
    col_base = owner * COLS
    scale = 1.0 / math.sqrt(slots * blocks * owners * 16)
    screen = make_screen(col_base.reshape(1), plane_w, scale)
    got = []
    for chunk in range(CHUNKS):
        coeffs = project_chunk(
            vis_count, kernel_u, kernel_v, visibilities, project, mark, owners, chunk, size
        )
        if chunk:
            coeffs, screen = lax.optimization_barrier((coeffs, screen))
        got.append(
            lax.all_to_all(coeffs, ("tu", "tv"), split_axis=0, concat_axis=0, tiled=True)
        )
    marks = got[0][:, MARK, : 4 * blocks].astype(jnp.int32).reshape(owners, 2, 2, blocks)
    corners = marks[:, :, 0] * 64 + marks[:, :, 1]
    rows = corners[:, 0, :].reshape(-1)
    cols = corners[:, 1, :].reshape(-1)

    lane = jnp.arange(COLS, dtype=jnp.int32)
    turns = (cols[:, None] * (col_base + lane)[None, :]) % N
    shift = (S - 1) / 2 * (lane.astype(jnp.float32) - (COLS - 1) / 2)
    angle = (turns.astype(jnp.float32) + shift[None, :]) * (2.0 * math.pi / N)
    phase = jnp.concatenate([jnp.cos(angle), jnp.sin(angle)], axis=1)

    me = lax.axis_index("wa")
    core, z_hi, x = me % 2, me // 2 % 2, me // 4
    step = jnp.arange(8, dtype=jnp.int32)
    pair = ((x + step // 2) % 4) * 4 + (z_hi ^ (step % 2)) * 2
    place = jnp.stack([pair + core, pair + (1 - core)])

    acc = grid_chunk(rows, got[0], phase, expand, 0, size, blocks)
    halves = make_image(
        rows, place, got[1], phase, expand, acc, table, screen, 1, size, blocks
    )
    if planes != 16:
        return halves
    even, odd = (sum_planes(keep, send, planes) for keep, send in halves)
    return jnp.stack([even, odd], axis=1).transpose(2, 0, 1, 3).reshape(L0 * 16, COLS)


def solution(mesh):
    split = ("wa", "tu", "tv")
    placed = (
        P(split, None, None),
        P(split, None, None),
        P(split, None, None),
        P(split),
        P(split, None),
        P(split, None),
        P("wa"),
    )
    return jax.shard_map(
        body, mesh=mesh, in_specs=placed, out_specs=P("wa", ("tu", "tv")), check_vma=False
    )
```

```python
import functools
import math

import jax
import jax.numpy as jnp
import ml_dtypes
import numpy as np
from jax import lax
from jax.experimental import pallas as pl
from jax.experimental.pallas import tpu as pltpu
from jax.sharding import PartitionSpec as P

N = 8192
HALF = 4096
S = 128
RANK = 15
STACK = 16
MARK = 15
KEPT = 80
COLS = 256
U0 = 512
U1 = 8
L0 = 16
L1 = 256
TILE = 1024
CHUNKS = 2
FIELD = 0.25
MIB = 1 << 20


def prolate(count, half_band):
    n = np.arange(S)
    diagonal = ((S - 1 - 2 * n) / 2) ** 2 * np.cos(2 * np.pi * half_band)
    beside = n[1:] * (S - n[1:]) / 2
    _, v = np.linalg.eigh(np.diag(diagonal) + np.diag(beside, 1) + np.diag(beside, -1))
    v = v[:, ::-1][:, :count]
    peak = np.argmax(np.abs(v[: S // 2]), axis=0)
    return v * np.sign(v[peak, np.arange(count)])


def factor_tables(owners):
    t = np.arange(S) - (S - 1) / 2
    mu = np.arange(COLS) - (COLS - 1) / 2
    basis = prolate(RANK, COLS / 2 / N)
    spread = basis.T @ np.exp(2j * np.pi * np.outer(t, mu) / N)
    pad = ((0, STACK - RANK), (0, 0))
    basis, spread = np.pad(basis.T, pad), np.pad(spread, pad)
    rows = []
    for j in range(owners):
        centre = COLS * j + (COLS - 1) / 2
        turn = np.exp(2j * np.pi * np.arange(S) * centre / N)
        proj = basis * turn[None, :]
        rows.append(np.concatenate([proj.real, -proj.imag], axis=1))
        rows.append(np.concatenate([proj.imag, proj.real], axis=1))
    project = np.concatenate(rows, axis=0).astype(ml_dtypes.bfloat16)
    sr, si = spread.real, spread.imag
    by_cos = np.block([[sr, si], [-si, sr]]).astype(np.float32)
    by_sin = np.block([[-si, sr], [-sr, -si]]).astype(np.float32)
    return project, np.stack([by_cos, by_sin])


def keep_table(size):
    v = prolate(KEPT, 0.25)
    return np.kron(np.eye(size), v).astype(ml_dtypes.bfloat16)


def row_table():
    u0 = np.arange(U0)[None, None, :]
    l0 = np.arange(L0)[:, None, None]
    l1 = np.arange(L1)[None, :, None]
    a = 2.0 * np.pi * ((u0 * (l0 + L0 * l1 - N // 4)) % N) / N
    c, s = np.cos(a).astype(ml_dtypes.bfloat16), np.sin(a).astype(ml_dtypes.bfloat16)
    table = np.concatenate(
        [np.concatenate([c, -s], axis=2), np.concatenate([s, c], axis=2)], axis=1
    )
    return table[0::2], table[1::2]


def project_kernel(
    count_ref, ku_ref, kv_ref, vis_ref, table_ref, keep_ref, mark_ref, out_ref, *, first
):
    slots = lax.broadcasted_iota(jnp.int32, (2, ku_ref.shape[1]), 1)
    owners, rows, width = out_ref.shape
    turn = lax.broadcasted_iota(jnp.int32, (1, S), 1) & 3
    cosine = jnp.where(turn == 0, 1.0, jnp.where(turn == 2, -1.0, 0.0))
    sine = jnp.where(turn == 1, 1.0, jnp.where(turn == 3, -1.0, 0.0))
    subs = []
    for b in range(ku_ref.shape[0]):
        live = count_ref[first + b]
        vis = jnp.where(slots < live, vis_ref[b].astype(jnp.float32), 0.0)
        kv_t = kv_ref[b].astype(jnp.float32).T
        weighted = jnp.concatenate([kv_t * vis[0:1, :], kv_t * vis[1:2, :]], axis=0)
        sub = jnp.dot(
            weighted.astype(jnp.bfloat16), ku_ref[b], preferred_element_type=jnp.float32
        )
        re, im = sub[:S], sub[S:]
        subs.append(
            jnp.concatenate(
                [re * cosine - im * sine, re * sine + im * cosine], axis=0
            ).astype(jnp.bfloat16)
        )
    table = table_ref[...]
    mark = jnp.concatenate([mark_ref[...], mark_ref[...]], axis=1)
    for lo in range(0, width, 256):
        hi = min(lo + 256, width)
        b0, b1 = lo // KEPT, -(-hi // KEPT)
        kept = jnp.dot(
            jnp.concatenate(subs[b0:b1], axis=1),
            keep_ref[b0 * S : b1 * S, lo:hi],
            preferred_element_type=jnp.float32,
        ).astype(jnp.bfloat16)
        out = jnp.dot(table, kept, preferred_element_type=jnp.float32)
        out = out.reshape(owners, rows, hi - lo)
        line = lax.broadcasted_iota(jnp.int32, (rows, hi - lo), 0)
        out = jnp.where((line == MARK)[None], mark[None, :, : hi - lo], out)
        out_ref[:, :, lo:hi] = out.astype(jnp.bfloat16)


def project_chunk(count, ku, kv, vis, table, keep, mark, owners, chunk, size):
    slots = ku.shape[1]
    return pl.pallas_call(
        functools.partial(project_kernel, first=chunk * size),
        out_shape=jax.ShapeDtypeStruct((owners, 2 * STACK, size * KEPT), jnp.bfloat16),
        grid_spec=pltpu.PrefetchScalarGridSpec(
            num_scalar_prefetch=1,
            grid=(1,),
            in_specs=[
                pl.BlockSpec((size, slots, S), lambda b, _: (chunk, 0, 0)),
                pl.BlockSpec((size, slots, S), lambda b, _: (chunk, 0, 0)),
                pl.BlockSpec((size, 2, slots), lambda b, _: (chunk, 0, 0)),
                pl.BlockSpec(table.shape, lambda b, _: (0, 0)),
                pl.BlockSpec(keep.shape, lambda b, _: (0, 0)),
                pl.BlockSpec(mark.shape, lambda b, _: (0, 0)),
            ],
            out_specs=pl.BlockSpec((owners, 2 * STACK, size * KEPT), lambda b, _: (0, 0, 0)),
        ),
        compiler_params=pltpu.CompilerParams(vmem_limit_bytes=60 * MIB),
        cost_estimate=pl.CostEstimate(
            flops=size * 2 * (256 * 256 * 128 + 512 * 256 * 128),
            bytes_accessed=size * 4 * 65536,
            transcendentals=0,
        ),
    )(count, ku, kv, vis, table, keep, mark)


def add_blocks(
    row_ref, got_ref, phase_ref, expand_ref, back_ref, coeff_ref, acc_ref, chunk, size, per_src
):
    sources, rows, width = got_ref.shape
    for g in range(size // 2):
        lo = 2 * KEPT * g // 128 * 128
        part = jnp.dot(
            got_ref[:, :, lo : lo + 256].reshape(sources * rows, 256),
            back_ref[lo : lo + 256, 256 * g : 256 * (g + 1)],
            preferred_element_type=jnp.float32,
        )
        coeff_ref[:, :, 256 * g : 256 * (g + 1)] = part.astype(jnp.bfloat16).reshape(
            sources, rows, 256
        )
    by_cos, by_sin = expand_ref[0], expand_ref[1]

    def per_source(src, carry):
        for b in range(size):
            g = src * per_src + chunk * size + b
            row = row_ref[g]
            ph = phase_ref[pl.ds(g, 1), :]
            c = jnp.concatenate([ph[:, :COLS], ph[:, :COLS]], axis=1)
            s = jnp.concatenate([ph[:, COLS:], ph[:, COLS:]], axis=1)
            weights = (by_cos * c + by_sin * s).astype(jnp.bfloat16)
            coeffs = coeff_ref[src, :, b * S : (b + 1) * S]
            block = lax.dot_general(
                coeffs, weights, (((0,), (0,)), ((), ())), preferred_element_type=jnp.float32
            )
            for q in range(4):
                acc_ref[q, pl.ds(row, S), :] += block[:, q * 128 : (q + 1) * 128]
        return carry

    lax.fori_loop(0, sources, per_source, 0, unroll=2)


def grid_kernel(
    row_ref, got_ref, phase_ref, expand_ref, back_ref, out_ref, coeff_ref, *, chunk, size, per_src
):
    out_ref[...] = jnp.zeros_like(out_ref)
    add_blocks(
        row_ref, got_ref, phase_ref, expand_ref, back_ref, coeff_ref, out_ref, chunk, size, per_src
    )


def coeff_scratch(got, size):
    return pltpu.VMEM((got.shape[0], got.shape[1], size * S), jnp.bfloat16)


def grid_chunk(rows, got, phase, expand, back, chunk, size, per_src):
    vmem = pl.BlockSpec(memory_space=pltpu.VMEM)
    return pl.pallas_call(
        functools.partial(grid_kernel, chunk=chunk, size=size, per_src=per_src),
        out_shape=jax.ShapeDtypeStruct((4, HALF, 128), jnp.float32),
        in_specs=[pl.BlockSpec(memory_space=pltpu.SMEM), vmem, vmem, vmem, vmem],
        out_specs=vmem,
        scratch_shapes=[coeff_scratch(got, size)],
        compiler_params=pltpu.CompilerParams(vmem_limit_bytes=56 * MIB),
        cost_estimate=pl.CostEstimate(
            flops=got.shape[0] * size * 2 * 128 * 256 * 512,
            bytes_accessed=12 * MIB,
            transcendentals=0,
        ),
    )(rows, got, phase, expand, back)


def dft8(x):
    def add(p, q):
        return (p[0] + q[0], p[1] + q[1])

    def sub(p, q):
        return (p[0] - q[0], p[1] - q[1])

    def turn(p):
        return (-p[1], p[0])

    def dft4(a, b, c, d):
        s, t, v, w = add(a, c), sub(a, c), add(b, d), turn(sub(b, d))
        return add(s, v), add(t, w), sub(s, v), sub(t, w)

    h = math.sqrt(0.5)
    e = dft4(x[0], x[2], x[4], x[6])
    o = list(dft4(x[1], x[3], x[5], x[7]))
    o[1] = ((o[1][0] - o[1][1]) * h, (o[1][0] + o[1][1]) * h)
    o[2] = turn(o[2])
    o[3] = ((-o[3][0] - o[3][1]) * h, (o[3][0] - o[3][1]) * h)
    return [add(e[k], o[k]) for k in range(4)] + [sub(e[k], o[k]) for k in range(4)]


def finish(place_ref, table_ref, mid_ref, screen_ref, full_ref, keep_ref, send_ref):
    def last_step(k, carry):
        planar = jnp.dot(table_ref[k], mid_ref[k], preferred_element_type=jnp.float32)
        value = planar[:L1] * screen_ref[k, 0] - planar[L1:] * screen_ref[k, 1]
        full_ref[:, k] = value.astype(jnp.bfloat16).reshape(L1 // 16, 16, COLS)
        return carry

    lax.fori_loop(0, L0 // 2, last_step, 0, unroll=4)
    for out_ref, which in ((keep_ref, 0), (send_ref, 1)):
        for i in range(out_ref.shape[0]):
            out_ref[i] = full_ref[place_ref[which, i]]


def even_kernel(
    row_ref, place_ref, got_ref, phase_ref, expand_ref, back_ref, old_hbm, table_hbm, screen_hbm,
    keep_ref, send_ref, odd_ref,
    coeff_ref, acc_ref, old_ref, table_ref, mid_ref, screen_ref, full_ref, sems,
    *, chunk, size, per_src,
):
    load_old = pltpu.make_async_copy(old_hbm, old_ref, sems.at[0])
    load_table = pltpu.make_async_copy(table_hbm, table_ref, sems.at[1])
    load_screen = pltpu.make_async_copy(screen_hbm, screen_ref, sems.at[2])
    load_old.start()
    load_table.start()
    load_screen.start()
    acc_ref[...] = jnp.zeros_like(acc_ref)
    add_blocks(
        row_ref, got_ref, phase_ref, expand_ref, back_ref, coeff_ref, acc_ref, chunk, size, per_src
    )
    load_old.wait()

    def first_step(i, carry):
        at = pl.multiple_of(i * 16, 16)
        for half in range(2):
            x = [
                tuple(
                    acc_ref[2 * p + half, pl.ds(at + U0 * k, 16), :]
                    + old_ref[2 * p + half, pl.ds(at + U0 * k, 16), :]
                    for p in range(2)
                )
                for k in range(U1)
            ]
            even = dft8(x)
            for k in range(1, U1):
                c, s = math.cos(math.pi * k / U1), math.sin(math.pi * k / U1)
                x[k] = (x[k][0] * c - x[k][1] * s, x[k][0] * s + x[k][1] * c)
            for ref, out in ((mid_ref, even), (odd_ref, dft8(x))):
                for k in range(L0 // 2):
                    for p in range(2):
                        ref[k, pl.ds(U0 * p + at, 16), half * 128 : (half + 1) * 128] = out[k][
                            p
                        ].astype(jnp.bfloat16)
        return carry

    lax.fori_loop(0, U0 // 16, first_step, 0)
    load_table.wait()
    load_screen.wait()
    finish(place_ref, table_ref, mid_ref, screen_ref, full_ref, keep_ref, send_ref)


def odd_kernel(
    place_ref, mid_ref, table_ref, screen_ref, keep_ref, send_ref, full_ref
):
    finish(place_ref, table_ref, mid_ref, screen_ref, full_ref, keep_ref, send_ref)


def make_image(
    rows, place, got, phase, expand, back, old, tables, screens, chunk, size, per_src
):
    vmem = pl.BlockSpec(memory_space=pltpu.VMEM)
    smem = pl.BlockSpec(memory_space=pltpu.SMEM)
    hbm = pl.BlockSpec(memory_space=pl.ANY)
    half = L0 // 2
    piece = jax.ShapeDtypeStruct((place.shape[1], half, 16, COLS), jnp.bfloat16)
    mid = (half, 2 * U0, COLS)
    buffers = [
        pltpu.VMEM(tables[0].shape, jnp.bfloat16),
        pltpu.VMEM(screens[0].shape, jnp.float32),
        pltpu.VMEM((16, half, 16, COLS), jnp.bfloat16),
    ]
    keep, send, odd = pl.pallas_call(
        functools.partial(even_kernel, chunk=chunk, size=size, per_src=per_src),
        out_shape=(piece, piece, jax.ShapeDtypeStruct(mid, jnp.bfloat16)),
        in_specs=[smem, smem, vmem, vmem, vmem, vmem, hbm, hbm, hbm],
        out_specs=(vmem, vmem, vmem),
        scratch_shapes=[
            coeff_scratch(got, size),
            pltpu.VMEM(old.shape, jnp.float32),
            pltpu.VMEM(old.shape, jnp.float32),
            buffers[0],
            pltpu.VMEM(mid, jnp.bfloat16),
            *buffers[1:],
            pltpu.SemaphoreType.DMA((3,)),
        ],
        compiler_params=pltpu.CompilerParams(vmem_limit_bytes=45 * MIB),
        cost_estimate=pl.CostEstimate(
            flops=16 * 1024**3, bytes_accessed=24 * MIB, transcendentals=0
        ),
    )(rows, place, got, phase, expand, back, old, tables[0], screens[0])
    keep_odd, send_odd = pl.pallas_call(
        odd_kernel,
        out_shape=(piece, piece),
        in_specs=[smem, vmem, vmem, vmem],
        out_specs=(vmem, vmem),
        scratch_shapes=[buffers[2]],
        compiler_params=pltpu.CompilerParams(vmem_limit_bytes=22 * MIB),
        cost_estimate=pl.CostEstimate(
            flops=4 * 1024**3, bytes_accessed=12 * MIB, transcendentals=0
        ),
    )(place, odd, tables[1], screens[1])
    return (keep, send), (keep_odd, send_odd)


def screen_kernel(base_ref, w_ref, even_ref, odd_ref, *, scale):
    cell = 2.0 * FIELD / N
    col = base_ref[0] + lax.broadcasted_iota(jnp.int32, (1, COLS), 1)
    dm = col.astype(jnp.float32) * cell
    h = math.pi / 2
    for half, out_ref in enumerate((even_ref, odd_ref)):
        l0 = 2 * pl.program_id(0) + half
        row = l0 + L0 * lax.broadcasted_iota(jnp.int32, (L1, 1), 0)
        dl = row.astype(jnp.float32) * cell
        lift = jnp.sqrt((1.0 - dl * dl) - dm * dm) - 1.0
        quarters = (4.0 * w_ref[0]) * lift
        whole = jnp.floor(quarters + 0.5)
        f = quarters - whole
        count = whole.astype(jnp.int32) - (row + col)
        t = f * f
        sine, cosine = 0.0, 0.0
        for n in (9, 7, 5, 3, 1):
            sine = sine * t + (-1) ** (n // 2) * h**n / math.factorial(n) * scale
        for n in (10, 8, 6, 4, 2, 0):
            cosine = cosine * t + (-1) ** (n // 2) * h**n / math.factorial(n) * scale
        sine = sine * f
        odd = (count & 1) == 1
        c = jnp.where(odd, sine, cosine)
        s = jnp.where(odd, cosine, sine)
        out_ref[0, 0] = jnp.where(((count + 1) & 2) == 2, -c, c)
        out_ref[0, 1] = jnp.where((count & 2) == 2, -s, s)


def make_screen(base, w, scale):
    smem = pl.BlockSpec(memory_space=pltpu.SMEM)
    half = jax.ShapeDtypeStruct((L0 // 2, 2, L1, COLS), jnp.float32)
    spec = pl.BlockSpec((1, 2, L1, COLS), lambda k: (k, 0, 0, 0))
    return pl.pallas_call(
        functools.partial(screen_kernel, scale=scale),
        out_shape=(half, half),
        grid=(L0 // 2,),
        in_specs=[smem, smem],
        out_specs=(spec, spec),
        compiler_params=pltpu.CompilerParams(vmem_limit_bytes=60 * MIB),
        cost_estimate=pl.CostEstimate(
            flops=40 * HALF * COLS, bytes_accessed=8 * MIB, transcendentals=HALF * COLS
        ),
    )(base, w)


def sum_planes(keep, send, planes):
    def shifted(values, target):
        pairs = [(i, target(i)) for i in range(planes)]
        return lax.ppermute(values, "wa", pairs).astype(jnp.float32)

    total = keep.astype(jnp.float32) + shifted(send, lambda i: i ^ 1)
    total = total.astype(jnp.bfloat16).reshape(4, 2, L0 // 2, 16, COLS)
    got = [
        shifted(total[step], lambda i, step=step: (i + 4 * step) % planes) for step in (1, 2, 3)
    ]
    total = (total[0].astype(jnp.float32) + got[0] + got[1] + got[2]).astype(jnp.bfloat16)
    return total[0].astype(jnp.float32) + shifted(total[1], lambda i: i ^ 2)


def body(kernel_u, kernel_v, visibilities, vis_count, tile_route, block_offset, plane_w):
    n_tu, n_tv, planes = lax.axis_size("tu"), lax.axis_size("tv"), lax.axis_size("wa")
    owners = n_tu * n_tv
    blocks, slots = kernel_u.shape[0], kernel_u.shape[1]
    size = blocks // CHUNKS
    project, expand = factor_tables(owners)
    tables = row_table()
    keep = keep_table(size)
    back = np.ascontiguousarray(keep.T)

    target = tile_route[:, 0]
    corner = jnp.stack(
        [target // n_tv * TILE + block_offset[:, 0], target % n_tv * TILE + block_offset[:, 1]],
        axis=0,
    )
    halves = jnp.stack([corner // 64, corner % 64], axis=1).reshape(1, 4 * blocks)
    mark = jnp.pad(halves, ((0, 0), (0, S - 4 * blocks))).astype(jnp.float32)
    owner = lax.axis_index(("tu", "tv"))
    col_base = owner * COLS
    scale = 1.0 / math.sqrt(slots * blocks * owners * 16)
    screens = make_screen(col_base.reshape(1), plane_w, scale)
    got = []
    for chunk in range(CHUNKS):
        coeffs = project_chunk(
            vis_count, kernel_u, kernel_v, visibilities, project, keep, mark, owners, chunk, size
        )
        if chunk:
            coeffs, screens = lax.optimization_barrier((coeffs, screens))
        got.append(
            lax.all_to_all(coeffs, ("tu", "tv"), split_axis=0, concat_axis=0, tiled=True)
        )
    marks = got[0][:, MARK, : 4 * blocks].astype(jnp.int32).reshape(owners, 2, 2, blocks)
    corners = marks[:, :, 0] * 64 + marks[:, :, 1]
    rows = corners[:, 0, :].reshape(-1)
    cols = corners[:, 1, :].reshape(-1)

    lane = jnp.arange(COLS, dtype=jnp.int32)
    turns = (cols[:, None] * (col_base + lane)[None, :] + N // 4 * rows[:, None]) % N
    shift = (S - 1) / 2 * (lane.astype(jnp.float32) - (COLS - 1) / 2)
    angle = (turns.astype(jnp.float32) + shift[None, :]) * (2.0 * math.pi / N)
    phase = jnp.concatenate([jnp.cos(angle), jnp.sin(angle)], axis=1)

    me = lax.axis_index("wa")
    core, z_hi, x = me % 2, me // 2 % 2, me // 4
    step = jnp.arange(8, dtype=jnp.int32)
    pair = ((x + step // 2) % 4) * 4 + (z_hi ^ (step % 2)) * 2
    place = jnp.stack([pair + core, pair + (1 - core)])

    acc = grid_chunk(rows, got[0], phase, expand, back, 0, size, blocks)
    halves = make_image(
        rows, place, got[1], phase, expand, back, acc, tables, screens, 1, size, blocks
    )
    if planes != 16:
        return halves
    even, odd = (sum_planes(keep, send, planes) for keep, send in halves)
    return jnp.stack([even, odd], axis=1).transpose(2, 0, 1, 3).reshape(L0 * 16, COLS)


def solution(mesh):
    split = ("wa", "tu", "tv")
    placed = (
        P(split, None, None),
        P(split, None, None),
        P(split, None, None),
        P(split),
        P(split, None),
        P(split, None),
        P("wa"),
    )
    return jax.shard_map(
        body, mesh=mesh, in_specs=placed, out_specs=P("wa", ("tu", "tv")), check_vma=False
    )
```

```python
import functools
import math

import jax
import jax.numpy as jnp
import ml_dtypes
import numpy as np
from jax import lax
from jax.experimental import pallas as pl
from jax.experimental.pallas import tpu as pltpu
from jax.sharding import PartitionSpec as P

N = 8192
HALF = 4096
S = 128
RANK = 14
ROWS = 2 * RANK
STACK = 32
PACKED = 144
MARK = 140
KEPT = 80
COLS = 256
U0 = 512
U1 = 8
L0 = 16
L1 = 256
TILE = 1024
CHUNKS = 2
FIELD = 0.25
MIB = 1 << 20
EVEN_MIB = 45
ODD_MIB = 22


def prolate(count, half_band):
    n = np.arange(S)
    diagonal = ((S - 1 - 2 * n) / 2) ** 2 * np.cos(2 * np.pi * half_band)
    beside = n[1:] * (S - n[1:]) / 2
    _, v = np.linalg.eigh(np.diag(diagonal) + np.diag(beside, 1) + np.diag(beside, -1))
    v = v[:, ::-1][:, :count]
    peak = np.argmax(np.abs(v[: S // 2]), axis=0)
    return v * np.sign(v[peak, np.arange(count)])


def factor_tables(owners):
    t = np.arange(S) - (S - 1) / 2
    mu = np.arange(COLS) - (COLS - 1) / 2
    basis = prolate(RANK, COLS / 2 / N)
    spread = basis.T @ np.exp(2j * np.pi * np.outer(t, mu) / N)
    project = []
    for pad in ((0, STACK - ROWS), (STACK - ROWS, 0)):
        rows = []
        for j in range(owners):
            centre = COLS * j + (COLS - 1) / 2
            turn = np.exp(2j * np.pi * np.arange(S) * centre / N)
            proj = basis.T * turn[None, :]
            rows.append(np.pad(np.block([[proj.real, -proj.imag], [proj.imag, proj.real]]), (pad, (0, 0))))
        project.append(np.concatenate(rows, axis=0))
    sr, si = spread.real, spread.imag
    pad = ((0, STACK - ROWS), (0, 0))
    by_cos = np.pad(np.block([[sr, si], [-si, sr]]), pad).astype(np.float32)
    by_sin = np.pad(np.block([[-si, sr], [-sr, -si]]), pad).astype(np.float32)
    return np.stack(project).astype(ml_dtypes.bfloat16), np.stack([by_cos, by_sin])


def keep_spans(size):
    width = size * KEPT
    runs = [(lo, min(lo + 256, width)) for lo in range(0, width, 256)]
    return [(lo, hi, lo // KEPT, -(-hi // KEPT)) for lo, hi in runs]


def keep_tables(size):
    whole = np.kron(np.eye(size), prolate(KEPT, 0.25)).astype(ml_dtypes.bfloat16)
    to = [
        np.pad(whole[b0 * S : b1 * S, lo:hi], ((0, 0), (0, 256 - (hi - lo))))
        for lo, hi, b0, b1 in keep_spans(size)
    ]
    back = []
    for g in range(size // 2):
        lo = 2 * KEPT * g // 128 * 128
        back.append(whole[2 * S * g : 2 * S * (g + 1), lo : lo + 256].T)
    return np.concatenate(to, axis=0), np.stack(back)


def row_tables():
    u0 = np.arange(U0)[None, None, :]
    l0 = np.arange(L0)[:, None, None]
    l1 = np.arange(L1)[None, :, None]
    a = 2.0 * np.pi * ((u0 * (l0 + L0 * l1 - N // 4)) % N) / N
    c, s = np.cos(a).astype(ml_dtypes.bfloat16), np.sin(a).astype(ml_dtypes.bfloat16)
    table = np.concatenate(
        [np.concatenate([c, -s], axis=2), np.concatenate([s, c], axis=2)], axis=1
    )
    return table[0::2], table[1::2]


def corner_marks(route_ref, offset_ref, n_tv):
    lane = lax.broadcasted_iota(jnp.int32, (1, S), 1)
    marks = jnp.zeros((1, S), jnp.int32)
    blocks = route_ref.shape[1]
    for b in range(blocks):
        tile = route_ref[0, b]
        place = (tile // n_tv, tile % n_tv)
        for axis in range(2):
            corner = place[axis] * TILE + offset_ref[axis, b]
            at = 2 * blocks * axis + b
            marks = jnp.where(lane == at, corner // 64, marks)
            marks = jnp.where(lane == at + blocks, corner % 64, marks)
    return marks.astype(jnp.float32)


def project_kernel(
    count_ref, route_ref, offset_ref, ku_ref, kv_ref, vis_ref, table_ref, keep_ref, out_ref,
    *, first, n_tv,
):
    slots = lax.broadcasted_iota(jnp.int32, (2, ku_ref.shape[1]), 1)
    owners, rows, _ = out_ref.shape
    turn = lax.broadcasted_iota(jnp.int32, (1, S), 1) & 3
    cosine = jnp.where(turn == 0, 1.0, jnp.where(turn == 2, -1.0, 0.0))
    sine = jnp.where(turn == 1, 1.0, jnp.where(turn == 3, -1.0, 0.0))
    subs = []
    for b in range(ku_ref.shape[0]):
        live = count_ref[first + b]
        vis = jnp.where(slots < live, vis_ref[b].astype(jnp.float32), 0.0)
        kv_t = kv_ref[b].astype(jnp.float32).T
        weighted = jnp.concatenate([kv_t * vis[0:1, :], kv_t * vis[1:2, :]], axis=0)
        sub = jnp.dot(
            weighted.astype(jnp.bfloat16), ku_ref[b], preferred_element_type=jnp.float32
        )
        re, im = sub[:S], sub[S:]
        subs.append(
            jnp.concatenate(
                [re * cosine - im * sine, re * sine + im * cosine], axis=0
            ).astype(jnp.bfloat16)
        )
    start, runs = 0, []
    for lo, hi, b0, b1 in keep_spans(ku_ref.shape[0]):
        depth = (b1 - b0) * S
        kept = jnp.dot(
            jnp.concatenate(subs[b0:b1], axis=1),
            keep_ref[start : start + depth, : hi - lo],
            preferred_element_type=jnp.float32,
        ).astype(jnp.bfloat16)
        start += depth
        runs += [kept[:, i : i + 128] for i in range(0, hi - lo, 128)]

    tiles = [None] * len(runs)
    for which in range(2):
        mine = list(range(which, len(runs), 2))
        for i in range(0, len(mine), 2):
            pair = mine[i : i + 2]
            out = jnp.dot(
                table_ref[which],
                jnp.concatenate([runs[t] for t in pair], axis=1),
                preferred_element_type=jnp.float32,
            ).reshape(owners, STACK, 128 * len(pair))
            for n, t in enumerate(pair):
                tiles[t] = out[:, :, 128 * n : 128 * (n + 1)]
    whole, part = ROWS // 8 * 8, STACK - ROWS
    pieces = []
    for t in range(0, len(tiles), 2):
        pieces.append(tiles[t][:, :whole])
        if t + 1 < len(tiles):
            pieces += [tiles[t][:, whole:] + tiles[t + 1][:, :8], tiles[t + 1][:, 8:]]
        else:
            line = lax.broadcasted_iota(jnp.int32, (8, S), 0)
            marks = corner_marks(route_ref, offset_ref, n_tv) if first == 0 else 0.0
            last = jnp.where((line == MARK % 8)[None], marks, tiles[t][:, whole:])
            pieces += [last, jnp.zeros((owners, rows - MARK // 8 * 8 - 8, S), jnp.float32)]
    pieces = [p for p in pieces if p.shape[1]]
    out_ref[...] = jnp.concatenate(pieces, axis=1).astype(jnp.bfloat16)


def project_chunk(count, route, offset, ku, kv, vis, table, keep, owners, n_tv, chunk, size):
    slots = ku.shape[1]
    return pl.pallas_call(
        functools.partial(project_kernel, first=chunk * size, n_tv=n_tv),
        out_shape=jax.ShapeDtypeStruct((owners, PACKED, S), jnp.bfloat16),
        grid_spec=pltpu.PrefetchScalarGridSpec(
            num_scalar_prefetch=3,
            grid=(1,),
            in_specs=[
                pl.BlockSpec((size, slots, S), lambda b, *_: (chunk, 0, 0)),
                pl.BlockSpec((size, slots, S), lambda b, *_: (chunk, 0, 0)),
                pl.BlockSpec((size, 2, slots), lambda b, *_: (chunk, 0, 0)),
                pl.BlockSpec(table.shape, lambda b, *_: (0, 0, 0)),
                pl.BlockSpec(keep.shape, lambda b, *_: (0, 0)),
            ],
            out_specs=pl.BlockSpec((owners, PACKED, S), lambda b, *_: (0, 0, 0)),
        ),
        compiler_params=pltpu.CompilerParams(vmem_limit_bytes=60 * MIB),
        cost_estimate=pl.CostEstimate(
            flops=size * 2 * (256 * 256 * 128 + 512 * 256 * 128),
            bytes_accessed=size * 4 * 65536,
            transcendentals=0,
        ),
    )(count, route, offset, ku, kv, vis, table, keep)


def add_blocks(
    row_ref, got_ref, phase_ref, expand_ref, back_ref, coeff_ref, acc_ref, chunk, size, per_src
):
    sources = got_ref.shape[0]
    packed = got_ref[...].astype(jnp.float32)
    blank = jnp.zeros((sources, STACK - ROWS, S), jnp.float32)
    tiles = [
        jnp.concatenate([packed[:, ROWS * t : ROWS * (t + 1)], blank], axis=1)
        .astype(jnp.bfloat16)
        .reshape(sources * STACK, S)
        for t in range(size * KEPT // S)
    ]
    for g in range(size // 2):
        t = 2 * KEPT * g // S
        part = jnp.dot(
            jnp.concatenate(tiles[t : t + 2], axis=1), back_ref[g], preferred_element_type=jnp.float32
        )
        coeff_ref[:, :, 256 * g : 256 * (g + 1)] = part.astype(jnp.bfloat16).reshape(
            sources, STACK, 256
        )
    by_cos, by_sin = expand_ref[0], expand_ref[1]

    def per_source(src, carry):
        for b in range(size):
            g = src * per_src + chunk * size + b
            row = row_ref[g]
            ph = phase_ref[pl.ds(g, 1), :]
            c = jnp.concatenate([ph[:, :COLS], ph[:, :COLS]], axis=1)
            s = jnp.concatenate([ph[:, COLS:], ph[:, COLS:]], axis=1)
            weights = (by_cos * c + by_sin * s).astype(jnp.bfloat16)
            coeffs = coeff_ref[src, :, b * S : (b + 1) * S]
            block = lax.dot_general(
                coeffs, weights, (((0,), (0,)), ((), ())), preferred_element_type=jnp.float32
            )
            for q in range(4):
                acc_ref[q, pl.ds(row, S), :] += block[:, q * 128 : (q + 1) * 128]
        return carry

    lax.fori_loop(0, sources, per_source, 0, unroll=2)


def grid_kernel(
    row_ref, got_ref, phase_ref, expand_ref, back_ref, out_ref, coeff_ref, *, chunk, size, per_src
):
    out_ref[...] = jnp.zeros_like(out_ref)
    add_blocks(
        row_ref, got_ref, phase_ref, expand_ref, back_ref, coeff_ref, out_ref, chunk, size, per_src
    )


def coeff_scratch(got, size):
    return pltpu.VMEM((got.shape[0], STACK, size * S), jnp.bfloat16)


def grid_chunk(rows, got, phase, expand, back, chunk, size, per_src):
    vmem = pl.BlockSpec(memory_space=pltpu.VMEM)
    return pl.pallas_call(
        functools.partial(grid_kernel, chunk=chunk, size=size, per_src=per_src),
        out_shape=jax.ShapeDtypeStruct((4, HALF, 128), jnp.float32),
        in_specs=[pl.BlockSpec(memory_space=pltpu.SMEM), vmem, vmem, vmem, vmem],
        out_specs=vmem,
        scratch_shapes=[coeff_scratch(got, size)],
        compiler_params=pltpu.CompilerParams(vmem_limit_bytes=56 * MIB),
        cost_estimate=pl.CostEstimate(
            flops=got.shape[0] * size * 2 * 128 * 256 * 512,
            bytes_accessed=12 * MIB,
            transcendentals=0,
        ),
    )(rows, got, phase, expand, back)


def dft8(x):
    def add(p, q):
        return (p[0] + q[0], p[1] + q[1])

    def sub(p, q):
        return (p[0] - q[0], p[1] - q[1])

    def turn(p):
        return (-p[1], p[0])

    def dft4(a, b, c, d):
        s, t, v, w = add(a, c), sub(a, c), add(b, d), turn(sub(b, d))
        return add(s, v), add(t, w), sub(s, v), sub(t, w)

    h = math.sqrt(0.5)
    e = dft4(x[0], x[2], x[4], x[6])
    o = list(dft4(x[1], x[3], x[5], x[7]))
    o[1] = ((o[1][0] - o[1][1]) * h, (o[1][0] + o[1][1]) * h)
    o[2] = turn(o[2])
    o[3] = ((-o[3][0] - o[3][1]) * h, (o[3][0] - o[3][1]) * h)
    return [add(e[k], o[k]) for k in range(4)] + [sub(e[k], o[k]) for k in range(4)]


def finish(place_ref, table_ref, mid_ref, screen_ref, full_ref, keep_ref, send_ref):
    def last_step(k, carry):
        planar = jnp.dot(table_ref[k], mid_ref[k], preferred_element_type=jnp.float32)
        value = planar[:L1] * screen_ref[k, 0] - planar[L1:] * screen_ref[k, 1]
        full_ref[:, k] = value.astype(jnp.bfloat16).reshape(L1 // 16, 16, COLS)
        return carry

    lax.fori_loop(0, L0 // 2, last_step, 0, unroll=4)
    for out_ref, which in ((keep_ref, 0), (send_ref, 1)):
        for i in range(out_ref.shape[0]):
            out_ref[i] = full_ref[place_ref[which, i]]


def even_kernel(
    row_ref, place_ref, got_ref, phase_ref, expand_ref, back_ref, old_hbm, table_hbm, screen_hbm,
    keep_ref, send_ref, odd_ref,
    coeff_ref, acc_ref, old_ref, table_ref, mid_ref, screen_ref, full_ref, sems,
    *, chunk, size, per_src,
):
    load_old = pltpu.make_async_copy(old_hbm, old_ref, sems.at[0])
    load_table = pltpu.make_async_copy(table_hbm, table_ref, sems.at[1])
    load_screen = pltpu.make_async_copy(screen_hbm, screen_ref, sems.at[2])
    load_old.start()
    load_table.start()
    load_screen.start()
    acc_ref[...] = jnp.zeros_like(acc_ref)
    add_blocks(
        row_ref, got_ref, phase_ref, expand_ref, back_ref, coeff_ref, acc_ref, chunk, size, per_src
    )
    load_old.wait()

    def first_step(i, carry):
        at = pl.multiple_of(i * 16, 16)
        for half in range(2):
            x = [
                tuple(
                    acc_ref[2 * p + half, pl.ds(at + U0 * k, 16), :]
                    + old_ref[2 * p + half, pl.ds(at + U0 * k, 16), :]
                    for p in range(2)
                )
                for k in range(U1)
            ]
            even = dft8(x)
            for k in range(1, U1):
                c, s = math.cos(math.pi * k / U1), math.sin(math.pi * k / U1)
                x[k] = (x[k][0] * c - x[k][1] * s, x[k][0] * s + x[k][1] * c)
            for ref, out in ((mid_ref, even), (odd_ref, dft8(x))):
                for k in range(L0 // 2):
                    for p in range(2):
                        ref[k, pl.ds(U0 * p + at, 16), half * 128 : (half + 1) * 128] = out[k][
                            p
                        ].astype(jnp.bfloat16)
        return carry

    lax.fori_loop(0, U0 // 16, first_step, 0)
    load_table.wait()
    load_screen.wait()
    finish(place_ref, table_ref, mid_ref, screen_ref, full_ref, keep_ref, send_ref)


def odd_kernel(
    place_ref, mid_ref, table_ref, screen_ref, keep_ref, send_ref, full_ref
):
    finish(place_ref, table_ref, mid_ref, screen_ref, full_ref, keep_ref, send_ref)


def make_image(
    rows, place, got, phase, expand, back, old, tables, screens, chunk, size, per_src
):
    vmem = pl.BlockSpec(memory_space=pltpu.VMEM)
    smem = pl.BlockSpec(memory_space=pltpu.SMEM)
    hbm = pl.BlockSpec(memory_space=pl.ANY)
    half = L0 // 2
    piece = jax.ShapeDtypeStruct((place.shape[1], half, 16, COLS), jnp.bfloat16)
    mid = (half, 2 * U0, COLS)
    buffers = [
        pltpu.VMEM(tables[0].shape, jnp.bfloat16),
        pltpu.VMEM(screens[0].shape, jnp.float32),
        pltpu.VMEM((16, half, 16, COLS), jnp.bfloat16),
    ]
    keep, send, odd = pl.pallas_call(
        functools.partial(even_kernel, chunk=chunk, size=size, per_src=per_src),
        out_shape=(piece, piece, jax.ShapeDtypeStruct(mid, jnp.bfloat16)),
        in_specs=[smem, smem, vmem, vmem, vmem, vmem, hbm, hbm, hbm],
        out_specs=(vmem, vmem, vmem),
        scratch_shapes=[
            coeff_scratch(got, size),
            pltpu.VMEM(old.shape, jnp.float32),
            pltpu.VMEM(old.shape, jnp.float32),
            buffers[0],
            pltpu.VMEM(mid, jnp.bfloat16),
            *buffers[1:],
            pltpu.SemaphoreType.DMA((3,)),
        ],
        compiler_params=pltpu.CompilerParams(vmem_limit_bytes=EVEN_MIB * MIB),
        cost_estimate=pl.CostEstimate(
            flops=16 * 1024**3, bytes_accessed=24 * MIB, transcendentals=0
        ),
    )(rows, place, got, phase, expand, back, old, tables[0], screens[0])
    keep_odd, send_odd = pl.pallas_call(
        odd_kernel,
        out_shape=(piece, piece),
        in_specs=[smem, vmem, vmem, vmem],
        out_specs=(vmem, vmem),
        scratch_shapes=[buffers[2]],
        compiler_params=pltpu.CompilerParams(vmem_limit_bytes=ODD_MIB * MIB),
        cost_estimate=pl.CostEstimate(
            flops=4 * 1024**3, bytes_accessed=12 * MIB, transcendentals=0
        ),
    )(place, odd, tables[1], screens[1])
    return (keep, send), (keep_odd, send_odd)


def screen_kernel(base_ref, w_ref, even_ref, odd_ref, *, scale):
    cell = 2.0 * FIELD / N
    col = base_ref[0] + lax.broadcasted_iota(jnp.int32, (1, COLS), 1)
    dm = col.astype(jnp.float32) * cell
    h = math.pi / 2
    for half, out_ref in enumerate((even_ref, odd_ref)):
        l0 = 2 * pl.program_id(0) + half
        row = l0 + L0 * lax.broadcasted_iota(jnp.int32, (L1, 1), 0)
        dl = row.astype(jnp.float32) * cell
        lift = jnp.sqrt((1.0 - dl * dl) - dm * dm) - 1.0
        quarters = (4.0 * w_ref[0]) * lift
        whole = jnp.floor(quarters + 0.5)
        f = quarters - whole
        count = whole.astype(jnp.int32) - (row + col)
        t = f * f
        sine, cosine = 0.0, 0.0
        for n in (9, 7, 5, 3, 1):
            sine = sine * t + (-1) ** (n // 2) * h**n / math.factorial(n) * scale
        for n in (10, 8, 6, 4, 2, 0):
            cosine = cosine * t + (-1) ** (n // 2) * h**n / math.factorial(n) * scale
        sine = sine * f
        odd = (count & 1) == 1
        c = jnp.where(odd, sine, cosine)
        s = jnp.where(odd, cosine, sine)
        out_ref[0, 0] = jnp.where(((count + 1) & 2) == 2, -c, c)
        out_ref[0, 1] = jnp.where((count & 2) == 2, -s, s)


def make_screen(base, w, scale):
    smem = pl.BlockSpec(memory_space=pltpu.SMEM)
    half = jax.ShapeDtypeStruct((L0 // 2, 2, L1, COLS), jnp.float32)
    spec = pl.BlockSpec((1, 2, L1, COLS), lambda k: (k, 0, 0, 0))
    return pl.pallas_call(
        functools.partial(screen_kernel, scale=scale),
        out_shape=(half, half),
        grid=(L0 // 2,),
        in_specs=[smem, smem],
        out_specs=(spec, spec),
        compiler_params=pltpu.CompilerParams(vmem_limit_bytes=60 * MIB),
        cost_estimate=pl.CostEstimate(
            flops=40 * HALF * COLS, bytes_accessed=8 * MIB, transcendentals=HALF * COLS
        ),
    )(base, w)


def sum_planes(keep, send, planes):
    def shifted(values, target):
        pairs = [(i, target(i)) for i in range(planes)]
        return lax.ppermute(values, "wa", pairs).astype(jnp.float32)

    total = keep.astype(jnp.float32) + shifted(send, lambda i: i ^ 1)
    total = total.astype(jnp.bfloat16).reshape(4, 2, L0 // 2, 16, COLS)
    got = [
        shifted(total[step], lambda i, step=step: (i + 4 * step) % planes) for step in (1, 2, 3)
    ]
    total = (total[0].astype(jnp.float32) + got[0] + got[1] + got[2]).astype(jnp.bfloat16)
    return total[0].astype(jnp.float32) + shifted(total[1], lambda i: i ^ 2)


def body(kernel_u, kernel_v, visibilities, vis_count, tile_route, block_offset, plane_w):
    n_tu, n_tv, planes = lax.axis_size("tu"), lax.axis_size("tv"), lax.axis_size("wa")
    owners = n_tu * n_tv
    blocks, slots = kernel_u.shape[0], kernel_u.shape[1]
    size = blocks // CHUNKS
    project, expand = factor_tables(owners)
    tables = row_tables()
    keep, back = keep_tables(size)

    owner = lax.axis_index(("tu", "tv"))
    col_base = owner * COLS
    scale = 1.0 / math.sqrt(slots * blocks * owners * 16)
    screens = make_screen(col_base.reshape(1), plane_w, scale)
    got = []
    for chunk in range(CHUNKS):
        coeffs = project_chunk(
            vis_count, tile_route.T, block_offset.T, kernel_u, kernel_v, visibilities, project, keep,
            owners, n_tv, chunk, size,
        )
        if chunk:
            coeffs, screens = lax.optimization_barrier((coeffs, screens))
        got.append(
            lax.all_to_all(coeffs, ("tu", "tv"), split_axis=0, concat_axis=0, tiled=True)
        )
    marks = got[0][:, MARK, : 4 * blocks].astype(jnp.int32).reshape(owners, 2, 2, blocks)
    corners = marks[:, :, 0] * 64 + marks[:, :, 1]
    rows = corners[:, 0, :].reshape(-1)
    cols = corners[:, 1, :].reshape(-1)

    lane = jnp.arange(COLS, dtype=jnp.int32)
    turns = (cols[:, None] * (col_base + lane)[None, :] + N // 4 * rows[:, None]) % N
    shift = (S - 1) / 2 * (lane.astype(jnp.float32) - (COLS - 1) / 2)
    angle = (turns.astype(jnp.float32) + shift[None, :]) * (2.0 * math.pi / N)
    phase = jnp.concatenate([jnp.cos(angle), jnp.sin(angle)], axis=1)

    me = lax.axis_index("wa")
    core, z_hi, x = me % 2, me // 2 % 2, me // 4
    step = jnp.arange(8, dtype=jnp.int32)
    pair = ((x + step // 2) % 4) * 4 + (z_hi ^ (step % 2)) * 2
    place = jnp.stack([pair + core, pair + (1 - core)])

    acc = grid_chunk(rows, got[0], phase, expand, back, 0, size, blocks)
    halves = make_image(
        rows, place, got[1], phase, expand, back, acc, tables, screens, 1, size, blocks
    )
    if planes != 16:
        return halves
    even, odd = (sum_planes(keep, send, planes) for keep, send in halves)
    return jnp.stack([even, odd], axis=1).transpose(2, 0, 1, 3).reshape(L0 * 16, COLS)


def solution(mesh):
    split = ("wa", "tu", "tv")
    placed = (
        P(split, None, None),
        P(split, None, None),
        P(split, None, None),
        P(split),
        P(split, None),
        P(split, None),
        P("wa"),
    )
    return jax.shard_map(
        body, mesh=mesh, in_specs=placed, out_specs=P("wa", ("tu", "tv")), check_vma=False
    )
```

```python
import functools
import math

import jax
import jax.numpy as jnp
import ml_dtypes
import numpy as np
from jax import lax
from jax.experimental import pallas as pl
from jax.experimental.pallas import tpu as pltpu
from jax.sharding import PartitionSpec as P

N = 8192
HALF = 4096
S = 128
RANK = 14
ROWS = 2 * RANK
STACK = 32
PACKED = 144
MARK = 140
KEPT = 80
PIECE = 2
COLS = 256
U0 = 512
U1 = 8
L0 = 16
L1 = 256
TILE = 1024
CHUNKS = 2
FIELD = 0.25
MIB = 1 << 20
EVEN_MIB = 45
ODD_MIB = 22


def prolate(count, half_band):
    n = np.arange(S)
    diagonal = ((S - 1 - 2 * n) / 2) ** 2 * np.cos(2 * np.pi * half_band)
    beside = n[1:] * (S - n[1:]) / 2
    _, v = np.linalg.eigh(np.diag(diagonal) + np.diag(beside, 1) + np.diag(beside, -1))
    v = v[:, ::-1][:, :count]
    peak = np.argmax(np.abs(v[: S // 2]), axis=0)
    return v * np.sign(v[peak, np.arange(count)])


def factor_tables(n_tu, n_tv):
    t = np.arange(S) - (S - 1) / 2
    mu = np.arange(COLS) - (COLS - 1) / 2
    basis = prolate(RANK, COLS / 2 / N)
    spread = basis.T @ np.exp(2j * np.pi * np.outer(t, mu) / N)
    project = []
    for pad in ((0, STACK - ROWS), (STACK - ROWS, 0)):
        rows = []
        for j in [tu * n_tv + tv for tv in range(n_tv) for tu in range(n_tu)]:
            centre = COLS * j + (COLS - 1) / 2
            turn = np.exp(2j * np.pi * np.arange(S) * centre / N)
            proj = basis.T * turn[None, :]
            rows.append(np.pad(np.block([[proj.real, -proj.imag], [proj.imag, proj.real]]), (pad, (0, 0))))
        project.append(np.concatenate(rows, axis=0))
    sr, si = spread.real, spread.imag
    pad = ((0, STACK - ROWS), (0, 0))
    by_cos = np.pad(np.block([[sr, si], [-si, sr]]), pad).astype(np.float32)
    by_sin = np.pad(np.block([[-si, sr], [-sr, -si]]), pad).astype(np.float32)
    return np.stack(project).astype(ml_dtypes.bfloat16), np.stack([by_cos, by_sin])


def keep_spans(size):
    width = size * KEPT
    runs = [(lo, min(lo + 256, width)) for lo in range(0, width, 256)]
    return [(lo, hi, lo // KEPT, -(-hi // KEPT)) for lo, hi in runs]


def keep_tables(size):
    whole = np.kron(np.eye(size), prolate(KEPT, 0.25)).astype(ml_dtypes.bfloat16)
    to = [
        np.pad(whole[b0 * S : b1 * S, lo:hi], ((0, 0), (0, 256 - (hi - lo))))
        for lo, hi, b0, b1 in keep_spans(size)
    ]
    back = []
    for g in range(size // 2):
        lo = 2 * KEPT * g // 128 * 128
        back.append(whole[2 * S * g : 2 * S * (g + 1), lo : lo + 256].T)
    return np.concatenate(to, axis=0), np.stack(back)


def row_tables():
    u0 = np.arange(U0)[None, None, :]
    l0 = np.arange(L0)[:, None, None]
    l1 = np.arange(L1)[None, :, None]
    a = 2.0 * np.pi * ((u0 * (l0 + L0 * l1 - N // 4)) % N) / N
    c, s = np.cos(a).astype(ml_dtypes.bfloat16), np.sin(a).astype(ml_dtypes.bfloat16)
    table = np.concatenate(
        [np.concatenate([c, -s], axis=2), np.concatenate([s, c], axis=2)], axis=1
    )
    return table[0::2], [table[k : 2 * PIECE + k : 2] for k in range(1, L0, 2 * PIECE)]


def corner_marks(route_ref, offset_ref, n_tv):
    lane = lax.broadcasted_iota(jnp.int32, (1, S), 1)
    marks = jnp.zeros((1, S), jnp.int32)
    blocks = route_ref.shape[1]
    for b in range(blocks):
        tile = route_ref[0, b]
        place = (tile // n_tv, tile % n_tv)
        for axis in range(2):
            corner = place[axis] * TILE + offset_ref[axis, b]
            at = 2 * blocks * axis + b
            marks = jnp.where(lane == at, corner // 64, marks)
            marks = jnp.where(lane == at + blocks, corner % 64, marks)
    return marks.astype(jnp.float32)


def project_kernel(
    count_ref, route_ref, offset_ref, ku_ref, kv_ref, vis_ref, table_ref, keep_ref, out_ref,
    *, first, n_tv,
):
    slots = lax.broadcasted_iota(jnp.int32, (2, ku_ref.shape[1]), 1)
    owners, rows, _ = out_ref.shape
    turn = lax.broadcasted_iota(jnp.int32, (1, S), 1) & 3
    cosine = jnp.where(turn == 0, 1.0, jnp.where(turn == 2, -1.0, 0.0))
    sine = jnp.where(turn == 1, 1.0, jnp.where(turn == 3, -1.0, 0.0))
    subs = []
    for b in range(ku_ref.shape[0]):
        live = count_ref[first + b]
        vis = jnp.where(slots < live, vis_ref[b].astype(jnp.float32), 0.0)
        kv_t = kv_ref[b].astype(jnp.float32).T
        weighted = jnp.concatenate([kv_t * vis[0:1, :], kv_t * vis[1:2, :]], axis=0)
        sub = jnp.dot(
            weighted.astype(jnp.bfloat16), ku_ref[b], preferred_element_type=jnp.float32
        )
        re, im = sub[:S], sub[S:]
        subs.append(
            jnp.concatenate(
                [re * cosine - im * sine, re * sine + im * cosine], axis=0
            ).astype(jnp.bfloat16)
        )
    start, runs = 0, []
    for lo, hi, b0, b1 in keep_spans(ku_ref.shape[0]):
        depth = (b1 - b0) * S
        kept = jnp.dot(
            jnp.concatenate(subs[b0:b1], axis=1),
            keep_ref[start : start + depth, : hi - lo],
            preferred_element_type=jnp.float32,
        ).astype(jnp.bfloat16)
        start += depth
        runs += [kept[:, i : i + 128] for i in range(0, hi - lo, 128)]

    tiles = [None] * len(runs)
    for which in range(2):
        mine = list(range(which, len(runs), 2))
        for i in range(0, len(mine), 2):
            pair = mine[i : i + 2]
            out = jnp.dot(
                table_ref[which],
                jnp.concatenate([runs[t] for t in pair], axis=1),
                preferred_element_type=jnp.float32,
            ).reshape(owners, STACK, 128 * len(pair))
            for n, t in enumerate(pair):
                tiles[t] = out[:, :, 128 * n : 128 * (n + 1)]
    whole, part = ROWS // 8 * 8, STACK - ROWS
    pieces = []
    for t in range(0, len(tiles), 2):
        pieces.append(tiles[t][:, :whole])
        if t + 1 < len(tiles):
            pieces += [tiles[t][:, whole:] + tiles[t + 1][:, :8], tiles[t + 1][:, 8:]]
        else:
            line = lax.broadcasted_iota(jnp.int32, (8, S), 0)
            marks = corner_marks(route_ref, offset_ref, n_tv) if first == 0 else 0.0
            last = jnp.where((line == MARK % 8)[None], marks, tiles[t][:, whole:])
            pieces += [last, jnp.zeros((owners, rows - MARK // 8 * 8 - 8, S), jnp.float32)]
    pieces = [p for p in pieces if p.shape[1]]
    out_ref[...] = jnp.concatenate(pieces, axis=1).astype(jnp.bfloat16)


def project_chunk(count, route, offset, ku, kv, vis, table, keep, owners, n_tv, chunk, size):
    slots = ku.shape[1]
    return pl.pallas_call(
        functools.partial(project_kernel, first=chunk * size, n_tv=n_tv),
        out_shape=jax.ShapeDtypeStruct((owners, PACKED, S), jnp.bfloat16),
        grid_spec=pltpu.PrefetchScalarGridSpec(
            num_scalar_prefetch=3,
            grid=(1,),
            in_specs=[
                pl.BlockSpec((size, slots, S), lambda b, *_: (chunk, 0, 0)),
                pl.BlockSpec((size, slots, S), lambda b, *_: (chunk, 0, 0)),
                pl.BlockSpec((size, 2, slots), lambda b, *_: (chunk, 0, 0)),
                pl.BlockSpec(table.shape, lambda b, *_: (0, 0, 0)),
                pl.BlockSpec(keep.shape, lambda b, *_: (0, 0)),
            ],
            out_specs=pl.BlockSpec((owners, PACKED, S), lambda b, *_: (0, 0, 0)),
        ),
        compiler_params=pltpu.CompilerParams(vmem_limit_bytes=60 * MIB),
        cost_estimate=pl.CostEstimate(
            flops=size * 2 * (256 * 256 * 128 + 512 * 256 * 128),
            bytes_accessed=size * 4 * 65536,
            transcendentals=0,
        ),
    )(count, route, offset, ku, kv, vis, table, keep)


def add_blocks(
    row_ref, got_ref, phase_ref, expand_ref, back_ref, coeff_ref, acc_ref, chunk, size, per_src
):
    sources = got_ref.shape[0]
    packed = got_ref[...].astype(jnp.float32)
    blank = jnp.zeros((sources, STACK - ROWS, S), jnp.float32)
    tiles = [
        jnp.concatenate([packed[:, ROWS * t : ROWS * (t + 1)], blank], axis=1)
        .astype(jnp.bfloat16)
        .reshape(sources * STACK, S)
        for t in range(size * KEPT // S)
    ]
    for g in range(size // 2):
        t = 2 * KEPT * g // S
        part = jnp.dot(
            jnp.concatenate(tiles[t : t + 2], axis=1), back_ref[g], preferred_element_type=jnp.float32
        )
        coeff_ref[:, :, 256 * g : 256 * (g + 1)] = part.astype(jnp.bfloat16).reshape(
            sources, STACK, 256
        )
    by_cos, by_sin = expand_ref[0], expand_ref[1]

    def per_source(src, carry):
        for b in range(size):
            g = src * per_src + chunk * size + b
            row = row_ref[g]
            ph = phase_ref[pl.ds(g, 1), :]
            c = jnp.concatenate([ph[:, :COLS], ph[:, :COLS]], axis=1)
            s = jnp.concatenate([ph[:, COLS:], ph[:, COLS:]], axis=1)
            weights = (by_cos * c + by_sin * s).astype(jnp.bfloat16)
            coeffs = coeff_ref[src, :, b * S : (b + 1) * S]
            block = lax.dot_general(
                coeffs, weights, (((0,), (0,)), ((), ())), preferred_element_type=jnp.float32
            )
            for q in range(4):
                acc_ref[q, pl.ds(row, S), :] += block[:, q * 128 : (q + 1) * 128]
        return carry

    lax.fori_loop(0, sources, per_source, 0, unroll=2)


def grid_kernel(
    row_ref, got_ref, phase_ref, expand_ref, back_ref, out_ref, coeff_ref, *, chunk, size, per_src
):
    out_ref[...] = jnp.zeros_like(out_ref)
    add_blocks(
        row_ref, got_ref, phase_ref, expand_ref, back_ref, coeff_ref, out_ref, chunk, size, per_src
    )


def coeff_scratch(got, size):
    return pltpu.VMEM((got.shape[0], STACK, size * S), jnp.bfloat16)


def grid_chunk(rows, got, phase, expand, back, chunk, size, per_src):
    vmem = pl.BlockSpec(memory_space=pltpu.VMEM)
    return pl.pallas_call(
        functools.partial(grid_kernel, chunk=chunk, size=size, per_src=per_src),
        out_shape=jax.ShapeDtypeStruct((4, HALF, 128), jnp.float32),
        in_specs=[pl.BlockSpec(memory_space=pltpu.SMEM), vmem, vmem, vmem, vmem],
        out_specs=vmem,
        scratch_shapes=[coeff_scratch(got, size)],
        compiler_params=pltpu.CompilerParams(vmem_limit_bytes=56 * MIB),
        cost_estimate=pl.CostEstimate(
            flops=got.shape[0] * size * 2 * 128 * 256 * 512,
            bytes_accessed=12 * MIB,
            transcendentals=0,
        ),
    )(rows, got, phase, expand, back)


def dft8(x):
    def add(p, q):
        return (p[0] + q[0], p[1] + q[1])

    def sub(p, q):
        return (p[0] - q[0], p[1] - q[1])

    def turn(p):
        return (-p[1], p[0])

    def dft4(a, b, c, d):
        s, t, v, w = add(a, c), sub(a, c), add(b, d), turn(sub(b, d))
        return add(s, v), add(t, w), sub(s, v), sub(t, w)

    h = math.sqrt(0.5)
    e = dft4(x[0], x[2], x[4], x[6])
    o = list(dft4(x[1], x[3], x[5], x[7]))
    o[1] = ((o[1][0] - o[1][1]) * h, (o[1][0] + o[1][1]) * h)
    o[2] = turn(o[2])
    o[3] = ((-o[3][0] - o[3][1]) * h, (o[3][0] - o[3][1]) * h)
    return [add(e[k], o[k]) for k in range(4)] + [sub(e[k], o[k]) for k in range(4)]


def finish(place_ref, table_refs, mid_ref, screen_ref, full_ref, keep_ref, send_ref):
    for k in range(L0 // 2):
        ref = table_refs[k // table_refs[0].shape[0]]
        planar = jnp.dot(
            ref[k % ref.shape[0]], mid_ref[k], preferred_element_type=jnp.float32
        )
        value = planar[:L1] * screen_ref[k, 0] - planar[L1:] * screen_ref[k, 1]
        full_ref[:, k] = value.astype(jnp.bfloat16).reshape(L1 // 16, 16, COLS)
    for out_ref, which in ((keep_ref, 0), (send_ref, 1)):
        for i in range(out_ref.shape[0]):
            out_ref[i] = full_ref[place_ref[which, i]]


def even_kernel(
    row_ref, place_ref, got_ref, phase_ref, expand_ref, back_ref, old_hbm, table_hbm, screen_hbm,
    keep_ref, send_ref, odd_ref,
    coeff_ref, acc_ref, old_ref, table_ref, mid_ref, screen_ref, full_ref, sems,
    *, chunk, size, per_src,
):
    load_old = pltpu.make_async_copy(old_hbm, old_ref, sems.at[0])
    load_table = pltpu.make_async_copy(table_hbm, table_ref, sems.at[1])
    load_screen = pltpu.make_async_copy(screen_hbm, screen_ref, sems.at[2])
    load_old.start()
    load_table.start()
    load_screen.start()
    acc_ref[...] = jnp.zeros_like(acc_ref)
    add_blocks(
        row_ref, got_ref, phase_ref, expand_ref, back_ref, coeff_ref, acc_ref, chunk, size, per_src
    )
    load_old.wait()

    def first_step(i, carry):
        at = pl.multiple_of(i * 16, 16)
        for half in range(2):
            x = [
                tuple(
                    acc_ref[2 * p + half, pl.ds(at + U0 * k, 16), :]
                    + old_ref[2 * p + half, pl.ds(at + U0 * k, 16), :]
                    for p in range(2)
                )
                for k in range(U1)
            ]
            even = dft8(x)
            for k in range(1, U1):
                c, s = math.cos(math.pi * k / U1), math.sin(math.pi * k / U1)
                x[k] = (x[k][0] * c - x[k][1] * s, x[k][0] * s + x[k][1] * c)
            for ref, out in ((mid_ref, even), (odd_ref, dft8(x))):
                for k in range(L0 // 2):
                    for p in range(2):
                        ref[k, pl.ds(U0 * p + at, 16), half * 128 : (half + 1) * 128] = out[k][
                            p
                        ].astype(jnp.bfloat16)
        return carry

    lax.fori_loop(0, U0 // 16, first_step, 0)
    load_table.wait()
    load_screen.wait()
    finish(place_ref, [table_ref], mid_ref, screen_ref, full_ref, keep_ref, send_ref)


def odd_kernel(place_ref, mid_ref, screen_ref, *refs):
    *table_refs, keep_ref, send_ref, full_ref = refs
    finish(place_ref, table_refs, mid_ref, screen_ref, full_ref, keep_ref, send_ref)


def make_image(
    rows, place, got, phase, expand, back, old, tables, screens, chunk, size, per_src
):
    vmem = pl.BlockSpec(memory_space=pltpu.VMEM)
    smem = pl.BlockSpec(memory_space=pltpu.SMEM)
    hbm = pl.BlockSpec(memory_space=pl.ANY)
    half = L0 // 2
    piece = jax.ShapeDtypeStruct((place.shape[1], half, 16, COLS), jnp.bfloat16)
    mid = (half, 2 * U0, COLS)
    buffers = [
        pltpu.VMEM(tables[0].shape, jnp.bfloat16),
        pltpu.VMEM(screens[0].shape, jnp.float32),
        pltpu.VMEM((16, half, 16, COLS), jnp.bfloat16),
    ]
    keep, send, odd = pl.pallas_call(
        functools.partial(even_kernel, chunk=chunk, size=size, per_src=per_src),
        out_shape=(piece, piece, jax.ShapeDtypeStruct(mid, jnp.bfloat16)),
        in_specs=[smem, smem, vmem, vmem, vmem, vmem, hbm, hbm, hbm],
        out_specs=(vmem, vmem, vmem),
        scratch_shapes=[
            coeff_scratch(got, size),
            pltpu.VMEM(old.shape, jnp.float32),
            pltpu.VMEM(old.shape, jnp.float32),
            buffers[0],
            pltpu.VMEM(mid, jnp.bfloat16),
            *buffers[1:],
            pltpu.SemaphoreType.DMA((3,)),
        ],
        compiler_params=pltpu.CompilerParams(vmem_limit_bytes=EVEN_MIB * MIB),
        cost_estimate=pl.CostEstimate(
            flops=16 * 1024**3, bytes_accessed=24 * MIB, transcendentals=0
        ),
    )(rows, place, got, phase, expand, back, old, tables[0], screens[0])
    keep_odd, send_odd = pl.pallas_call(
        odd_kernel,
        out_shape=(piece, piece),
        in_specs=[smem, *[vmem] * (2 + len(tables[1]))],
        out_specs=(vmem, vmem),
        scratch_shapes=[buffers[2]],
        compiler_params=pltpu.CompilerParams(vmem_limit_bytes=ODD_MIB * MIB),
        cost_estimate=pl.CostEstimate(
            flops=4 * 1024**3, bytes_accessed=12 * MIB, transcendentals=0
        ),
    )(place, odd, screens[1], *tables[1])
    return (keep, send), (keep_odd, send_odd)


def screen_kernel(base_ref, w_ref, even_ref, odd_ref, *, scale):
    cell = 2.0 * FIELD / N
    col = base_ref[0] + lax.broadcasted_iota(jnp.int32, (1, COLS), 1)
    dm = col.astype(jnp.float32) * cell
    h = math.pi / 2
    for half, out_ref in enumerate((even_ref, odd_ref)):
        l0 = 2 * pl.program_id(0) + half
        row = l0 + L0 * lax.broadcasted_iota(jnp.int32, (L1, 1), 0)
        dl = row.astype(jnp.float32) * cell
        lift = jnp.sqrt((1.0 - dl * dl) - dm * dm) - 1.0
        quarters = (4.0 * w_ref[0]) * lift
        whole = jnp.floor(quarters + 0.5)
        f = quarters - whole
        count = whole.astype(jnp.int32) - (row + col)
        t = f * f
        sine, cosine = 0.0, 0.0
        for n in (9, 7, 5, 3, 1):
            sine = sine * t + (-1) ** (n // 2) * h**n / math.factorial(n) * scale
        for n in (10, 8, 6, 4, 2, 0):
            cosine = cosine * t + (-1) ** (n // 2) * h**n / math.factorial(n) * scale
        sine = sine * f
        odd = (count & 1) == 1
        c = jnp.where(odd, sine, cosine)
        s = jnp.where(odd, cosine, sine)
        out_ref[0, 0] = jnp.where(((count + 1) & 2) == 2, -c, c)
        out_ref[0, 1] = jnp.where((count & 2) == 2, -s, s)


def make_screen(base, w, scale):
    smem = pl.BlockSpec(memory_space=pltpu.SMEM)
    half = jax.ShapeDtypeStruct((L0 // 2, 2, L1, COLS), jnp.float32)
    spec = pl.BlockSpec((1, 2, L1, COLS), lambda k: (k, 0, 0, 0))
    return pl.pallas_call(
        functools.partial(screen_kernel, scale=scale),
        out_shape=(half, half),
        grid=(L0 // 2,),
        in_specs=[smem, smem],
        out_specs=(spec, spec),
        compiler_params=pltpu.CompilerParams(vmem_limit_bytes=60 * MIB),
        cost_estimate=pl.CostEstimate(
            flops=40 * HALF * COLS, bytes_accessed=8 * MIB, transcendentals=HALF * COLS
        ),
    )(base, w)


def sum_planes(keep, send, planes):
    def shifted(values, target):
        pairs = [(i, target(i)) for i in range(planes)]
        return lax.ppermute(values, "wa", pairs).astype(jnp.float32)

    total = keep.astype(jnp.float32) + shifted(send, lambda i: i ^ 1)
    total = total.astype(jnp.bfloat16).reshape(4, 2, L0 // 2, 16, COLS)
    got = [
        shifted(total[step], lambda i, step=step: (i + 4 * step) % planes) for step in (1, 2, 3)
    ]
    total = (total[0].astype(jnp.float32) + got[0] + got[1] + got[2]).astype(jnp.bfloat16)
    return total[0].astype(jnp.float32) + shifted(total[1], lambda i: i ^ 2)


def body(kernel_u, kernel_v, visibilities, vis_count, tile_route, block_offset, plane_w):
    n_tu, n_tv, planes = lax.axis_size("tu"), lax.axis_size("tv"), lax.axis_size("wa")
    owners = n_tu * n_tv
    blocks, slots = kernel_u.shape[0], kernel_u.shape[1]
    size = blocks // CHUNKS
    project, expand = factor_tables(n_tu, n_tv)
    tables = row_tables()
    keep, back = keep_tables(size)

    owner = lax.axis_index(("tu", "tv"))
    col_base = owner * COLS
    scale = 1.0 / math.sqrt(slots * blocks * owners * 16)
    screens = make_screen(col_base.reshape(1), plane_w, scale)
    got = []
    for chunk in range(CHUNKS):
        coeffs = project_chunk(
            vis_count, tile_route.T, block_offset.T, kernel_u, kernel_v, visibilities, project, keep,
            owners, n_tv, chunk, size,
        )
        if chunk:
            coeffs, screens = lax.optimization_barrier((coeffs, screens))
        got.append(
            lax.all_to_all(coeffs, ("tv", "tu"), split_axis=0, concat_axis=0, tiled=True)
        )
    marks = got[0][:, MARK, : 4 * blocks].astype(jnp.int32).reshape(owners, 2, 2, blocks)
    corners = marks[:, :, 0] * 64 + marks[:, :, 1]
    rows = corners[:, 0, :].reshape(-1)
    cols = corners[:, 1, :].reshape(-1)

    lane = jnp.arange(COLS, dtype=jnp.int32)
    turns = (cols[:, None] * (col_base + lane)[None, :] + N // 4 * rows[:, None]) % N
    shift = (S - 1) / 2 * (lane.astype(jnp.float32) - (COLS - 1) / 2)
    angle = (turns.astype(jnp.float32) + shift[None, :]) * (2.0 * math.pi / N)
    phase = jnp.concatenate([jnp.cos(angle), jnp.sin(angle)], axis=1)

    me = lax.axis_index("wa")
    core, z_hi, x = me % 2, me // 2 % 2, me // 4
    step = jnp.arange(8, dtype=jnp.int32)
    pair = ((x + step // 2) % 4) * 4 + (z_hi ^ (step % 2)) * 2
    place = jnp.stack([pair + core, pair + (1 - core)])

    acc = grid_chunk(rows, got[0], phase, expand, back, 0, size, blocks)
    halves = make_image(
        rows, place, got[1], phase, expand, back, acc, tables, screens, 1, size, blocks
    )
    if planes != 16:
        return halves
    even, odd = (sum_planes(keep, send, planes) for keep, send in halves)
    return jnp.stack([even, odd], axis=1).transpose(2, 0, 1, 3).reshape(L0 * 16, COLS)


def solution(mesh):
    split = ("wa", "tu", "tv")
    placed = (
        P(split, None, None),
        P(split, None, None),
        P(split, None, None),
        P(split),
        P(split, None),
        P(split, None),
        P("wa"),
    )
    return jax.shard_map(
        body, mesh=mesh, in_specs=placed, out_specs=P("wa", ("tu", "tv")), check_vma=False
    )
```

```python
import functools
import math

import jax
import jax.numpy as jnp
import ml_dtypes
import numpy as np
from jax import lax
from jax.experimental import pallas as pl
from jax.experimental.pallas import tpu as pltpu
from jax.sharding import PartitionSpec as P

N = 8192
HALF = 4096
S = 128
RANK = 14
ROWS = 2 * RANK
STACK = 32
PACKED = 144
MARK = 140
KEPT = 80
PIECE = 1
COLS = 256
U0 = 512
U1 = 8
L0 = 16
L1 = 256
TILE = 1024
CHUNKS = 2
FIELD = 0.25
MIB = 1 << 20
EVEN_MIB = 45
ODD_MIB = 22


def prolate(count, half_band):
    n = np.arange(S)
    diagonal = ((S - 1 - 2 * n) / 2) ** 2 * np.cos(2 * np.pi * half_band)
    beside = n[1:] * (S - n[1:]) / 2
    _, v = np.linalg.eigh(np.diag(diagonal) + np.diag(beside, 1) + np.diag(beside, -1))
    v = v[:, ::-1][:, :count]
    peak = np.argmax(np.abs(v[: S // 2]), axis=0)
    return v * np.sign(v[peak, np.arange(count)])


def factor_tables(n_tu, n_tv):
    t = np.arange(S) - (S - 1) / 2
    mu = np.arange(COLS) - (COLS - 1) / 2
    basis = prolate(RANK, COLS / 2 / N)
    spread = basis.T @ np.exp(2j * np.pi * np.outer(t, mu) / N)
    project = []
    for pad in ((0, STACK - ROWS), (STACK - ROWS, 0)):
        rows = []
        for j in [tu * n_tv + tv for tv in range(n_tv) for tu in range(n_tu)]:
            centre = COLS * j + (COLS - 1) / 2
            turn = np.exp(2j * np.pi * np.arange(S) * centre / N)
            proj = basis.T * turn[None, :]
            rows.append(np.pad(np.block([[proj.real, -proj.imag], [proj.imag, proj.real]]), (pad, (0, 0))))
        project.append(np.concatenate(rows, axis=0))
    sr, si = spread.real, spread.imag
    pad = ((0, STACK - ROWS), (0, 0))
    by_cos = np.pad(np.block([[sr, si], [-si, sr]]), pad).astype(np.float32)
    by_sin = np.pad(np.block([[-si, sr], [-sr, -si]]), pad).astype(np.float32)
    return np.stack(project).astype(ml_dtypes.bfloat16), np.stack([by_cos, by_sin])


def keep_spans(size):
    width = size * KEPT
    runs = [(lo, min(lo + 256, width)) for lo in range(0, width, 256)]
    return [(lo, hi, lo // KEPT, -(-hi // KEPT)) for lo, hi in runs]


def keep_tables(size):
    whole = np.kron(np.eye(size), prolate(KEPT, 0.25)).astype(ml_dtypes.bfloat16)
    to = [
        np.pad(whole[b0 * S : b1 * S, lo:hi], ((0, 0), (0, 256 - (hi - lo))))
        for lo, hi, b0, b1 in keep_spans(size)
    ]
    back = []
    for g in range(size // 2):
        lo = 2 * KEPT * g // 128 * 128
        back.append(whole[2 * S * g : 2 * S * (g + 1), lo : lo + 256].T)
    return np.concatenate(to, axis=0), np.concatenate(back, axis=1)


def row_tables():
    u0 = np.arange(U0)[None, None, :]
    l0 = np.arange(L0)[:, None, None]
    l1 = np.arange(L1)[None, :, None]
    a = 2.0 * np.pi * ((u0 * (l0 + L0 * l1 - N // 4)) % N) / N
    c, s = np.cos(a).astype(ml_dtypes.bfloat16), np.sin(a).astype(ml_dtypes.bfloat16)
    table = np.concatenate(
        [np.concatenate([c, -s], axis=2), np.concatenate([s, c], axis=2)], axis=1
    )
    return table[0::2], [table[k : 2 * PIECE + k : 2] for k in range(1, L0, 2 * PIECE)]


def turned(quarters, back, scale):
    h = math.pi / 2
    whole = jnp.floor(quarters + 0.5)
    f = quarters - whole
    count = whole.astype(jnp.int32) - back
    t = f * f
    sine, cosine = 0.0, 0.0
    for n in (9, 7, 5, 3, 1):
        sine = sine * t + (-1) ** (n // 2) * h**n / math.factorial(n) * scale
    for n in (10, 8, 6, 4, 2, 0):
        cosine = cosine * t + (-1) ** (n // 2) * h**n / math.factorial(n) * scale
    sine = sine * f
    odd = (count & 1) == 1
    c = jnp.where(odd, sine, cosine)
    s = jnp.where(odd, cosine, sine)
    return (
        jnp.where(((count + 1) & 2) == 2, -c, c),
        jnp.where((count & 2) == 2, -s, s),
    )


def corner_marks(route_ref, offset_ref, n_tv):
    lane = lax.broadcasted_iota(jnp.int32, (1, S), 1)
    marks = jnp.zeros((1, S), jnp.int32)
    blocks = route_ref.shape[1]
    for b in range(blocks):
        tile = route_ref[0, b]
        place = (tile // n_tv, tile % n_tv)
        for axis in range(2):
            corner = place[axis] * TILE + offset_ref[axis, b]
            at = 2 * blocks * axis + b
            marks = jnp.where(lane == at, corner // 64, marks)
            marks = jnp.where(lane == at + blocks, corner % 64, marks)
    return marks.astype(jnp.float32)


def project_kernel(
    count_ref, route_ref, offset_ref, ku_ref, kv_ref, vis_ref, table_ref, keep_ref, out_ref,
    *, first, n_tv,
):
    slots = lax.broadcasted_iota(jnp.int32, (2, ku_ref.shape[1]), 1)
    owners, rows, _ = out_ref.shape
    turn = lax.broadcasted_iota(jnp.int32, (1, S), 1) & 3
    cosine = jnp.where(turn == 0, 1.0, jnp.where(turn == 2, -1.0, 0.0))
    sine = jnp.where(turn == 1, 1.0, jnp.where(turn == 3, -1.0, 0.0))
    subs = []
    for b in range(ku_ref.shape[0]):
        live = count_ref[first + b]
        vis = jnp.where(slots < live, vis_ref[b].astype(jnp.float32), 0.0)
        kv_t = kv_ref[b].astype(jnp.float32).T
        weighted = jnp.concatenate([kv_t * vis[0:1, :], kv_t * vis[1:2, :]], axis=0)
        sub = jnp.dot(
            weighted.astype(jnp.bfloat16), ku_ref[b], preferred_element_type=jnp.float32
        )
        re, im = sub[:S], sub[S:]
        subs.append(
            jnp.concatenate(
                [re * cosine - im * sine, re * sine + im * cosine], axis=0
            ).astype(jnp.bfloat16)
        )
    start, runs = 0, []
    for lo, hi, b0, b1 in keep_spans(ku_ref.shape[0]):
        depth = (b1 - b0) * S
        kept = jnp.dot(
            jnp.concatenate(subs[b0:b1], axis=1),
            keep_ref[start : start + depth, : hi - lo],
            preferred_element_type=jnp.float32,
        ).astype(jnp.bfloat16)
        start += depth
        runs += [kept[:, i : i + 128] for i in range(0, hi - lo, 128)]

    tiles = [None] * len(runs)
    for which in range(2):
        mine = list(range(which, len(runs), 2))
        for i in range(0, len(mine), 2):
            pair = mine[i : i + 2]
            out = jnp.dot(
                table_ref[which],
                jnp.concatenate([runs[t] for t in pair], axis=1),
                preferred_element_type=jnp.float32,
            ).reshape(owners, STACK, 128 * len(pair))
            for n, t in enumerate(pair):
                tiles[t] = out[:, :, 128 * n : 128 * (n + 1)]
    whole, part = ROWS // 8 * 8, STACK - ROWS
    pieces = []
    for t in range(0, len(tiles), 2):
        pieces.append(tiles[t][:, :whole])
        if t + 1 < len(tiles):
            pieces += [tiles[t][:, whole:] + tiles[t + 1][:, :8], tiles[t + 1][:, 8:]]
        else:
            line = lax.broadcasted_iota(jnp.int32, (8, S), 0)
            marks = corner_marks(route_ref, offset_ref, n_tv) if first == 0 else 0.0
            last = jnp.where((line == MARK % 8)[None], marks, tiles[t][:, whole:])
            pieces += [last, jnp.zeros((owners, rows - MARK // 8 * 8 - 8, S), jnp.float32)]
    pieces = [p for p in pieces if p.shape[1]]
    out_ref[...] = jnp.concatenate(pieces, axis=1).astype(jnp.bfloat16)


def project_chunk(count, route, offset, ku, kv, vis, table, keep, owners, n_tv, chunk, size):
    slots = ku.shape[1]
    return pl.pallas_call(
        functools.partial(project_kernel, first=chunk * size, n_tv=n_tv),
        out_shape=jax.ShapeDtypeStruct((owners, PACKED, S), jnp.bfloat16),
        grid_spec=pltpu.PrefetchScalarGridSpec(
            num_scalar_prefetch=3,
            grid=(1,),
            in_specs=[
                pl.BlockSpec((size, slots, S), lambda b, *_: (chunk, 0, 0)),
                pl.BlockSpec((size, slots, S), lambda b, *_: (chunk, 0, 0)),
                pl.BlockSpec((size, 2, slots), lambda b, *_: (chunk, 0, 0)),
                pl.BlockSpec(table.shape, lambda b, *_: (0, 0, 0)),
                pl.BlockSpec(keep.shape, lambda b, *_: (0, 0)),
            ],
            out_specs=pl.BlockSpec((owners, PACKED, S), lambda b, *_: (0, 0, 0)),
        ),
        compiler_params=pltpu.CompilerParams(vmem_limit_bytes=60 * MIB),
        cost_estimate=pl.CostEstimate(
            flops=size * 2 * (256 * 256 * 128 + 512 * 256 * 128),
            bytes_accessed=size * 4 * 65536,
            transcendentals=0,
        ),
    )(count, route, offset, ku, kv, vis, table, keep)


def add_blocks(
    row_ref, got_ref, phase_ref, expand_ref, back_ref, coeff_ref, acc_ref, size
):
    sources = got_ref.shape[0]
    packed = got_ref[...].astype(jnp.float32)
    blank = jnp.zeros((sources, STACK - ROWS, S), jnp.float32)
    tiles = [
        jnp.concatenate([packed[:, ROWS * t : ROWS * (t + 1)], blank], axis=1)
        .astype(jnp.bfloat16)
        .reshape(sources * STACK, S)
        for t in range(size * KEPT // S)
    ]
    for g in range(size // 2):
        t = 2 * KEPT * g // S
        part = jnp.dot(
            jnp.concatenate(tiles[t : t + 2], axis=1),
            back_ref[:, 256 * g : 256 * (g + 1)],
            preferred_element_type=jnp.float32,
        )
        coeff_ref[:, :, 256 * g : 256 * (g + 1)] = part.astype(jnp.bfloat16).reshape(
            sources, STACK, 256
        )
    by_cos, by_sin = expand_ref[0], expand_ref[1]

    lane = lax.broadcasted_iota(jnp.int32, (1, COLS), 1)
    centre = (S - 1) / 2 * (lane.astype(jnp.float32) - (COLS - 1) / 2)

    def per_source(src, carry):
        base = phase_ref[pl.ds(pl.multiple_of(src * size, size), size), :]
        turns = (base[:, 0:1] * lane + base[:, 1:2]) & (N - 1)
        phases = jnp.concatenate(
            turned((turns.astype(jnp.float32) + centre) * (4.0 / N), 0, 1.0), axis=1
        )
        for b in range(size):
            row = row_ref[src * size + b]
            ph = phases[b : b + 1]
            c = jnp.concatenate([ph[:, :COLS], ph[:, :COLS]], axis=1)
            s = jnp.concatenate([ph[:, COLS:], ph[:, COLS:]], axis=1)
            weights = (by_cos * c + by_sin * s).astype(jnp.bfloat16)
            coeffs = coeff_ref[src, :, b * S : (b + 1) * S]
            block = lax.dot_general(
                coeffs, weights, (((0,), (0,)), ((), ())), preferred_element_type=jnp.float32
            )
            for q in range(4):
                acc_ref[q, pl.ds(row, S), :] += block[:, q * 128 : (q + 1) * 128]
        return carry

    lax.fori_loop(0, sources, per_source, 0, unroll=4)


def grid_kernel(
    row_ref, got_ref, phase_ref, expand_ref, back_ref, out_ref, coeff_ref, *, size
):
    out_ref[...] = jnp.zeros_like(out_ref)
    add_blocks(
        row_ref, got_ref, phase_ref, expand_ref, back_ref, coeff_ref, out_ref, size
    )


def coeff_scratch(got, size):
    return pltpu.VMEM((got.shape[0], STACK, size * S), jnp.bfloat16)


def grid_chunk(rows, got, phase, expand, back, size):
    vmem = pl.BlockSpec(memory_space=pltpu.VMEM)
    return pl.pallas_call(
        functools.partial(grid_kernel, size=size),
        out_shape=jax.ShapeDtypeStruct((4, HALF, 128), jnp.float32),
        in_specs=[pl.BlockSpec(memory_space=pltpu.SMEM), vmem, vmem, vmem, vmem],
        out_specs=vmem,
        scratch_shapes=[coeff_scratch(got, size)],
        compiler_params=pltpu.CompilerParams(vmem_limit_bytes=56 * MIB),
        cost_estimate=pl.CostEstimate(
            flops=got.shape[0] * size * 2 * 128 * 256 * 512,
            bytes_accessed=12 * MIB,
            transcendentals=0,
        ),
    )(rows, got, phase, expand, back)


def dft8(x):
    def add(p, q):
        return (p[0] + q[0], p[1] + q[1])

    def sub(p, q):
        return (p[0] - q[0], p[1] - q[1])

    def turn(p):
        return (-p[1], p[0])

    def dft4(a, b, c, d):
        s, t, v, w = add(a, c), sub(a, c), add(b, d), turn(sub(b, d))
        return add(s, v), add(t, w), sub(s, v), sub(t, w)

    h = math.sqrt(0.5)
    e = dft4(x[0], x[2], x[4], x[6])
    o = list(dft4(x[1], x[3], x[5], x[7]))
    o[1] = ((o[1][0] - o[1][1]) * h, (o[1][0] + o[1][1]) * h)
    o[2] = turn(o[2])
    o[3] = ((-o[3][0] - o[3][1]) * h, (o[3][0] - o[3][1]) * h)
    return [add(e[k], o[k]) for k in range(4)] + [sub(e[k], o[k]) for k in range(4)]


def finish(place_ref, table_refs, mid_ref, screen_ref, full_ref, keep_ref, send_ref):
    for k in range(L0 // 2):
        ref = table_refs[k // table_refs[0].shape[0]]
        planar = jnp.dot(
            ref[k % ref.shape[0]], mid_ref[k], preferred_element_type=jnp.float32
        )
        c, s = (screen_ref[k, p].astype(jnp.float32) for p in range(2))
        value = planar[:L1] * c - planar[L1:] * s
        full_ref[:, k] = value.astype(jnp.bfloat16).reshape(L1 // 16, 16, COLS)
    for out_ref, which in ((keep_ref, 0), (send_ref, 1)):
        for i in range(out_ref.shape[0]):
            out_ref[i] = full_ref[place_ref[which, i]]


def even_kernel(
    row_ref, place_ref, got_ref, phase_ref, expand_ref, old_hbm, table_hbm, screen_hbm,
    keep_ref, send_ref, odd_ref,
    back_ref, coeff_ref, acc_ref, old_ref, table_ref, mid_ref, screen_ref, full_ref, sems,
    *, size,
):
    load_old = pltpu.make_async_copy(old_hbm, old_ref, sems.at[0])
    half = L0 // 2
    load_back = pltpu.make_async_copy(
        table_hbm.at[half, pl.ds(0, back_ref.shape[0])], back_ref, sems.at[3]
    )
    load_back.start()
    load_table = pltpu.make_async_copy(table_hbm.at[pl.ds(0, half)], table_ref, sems.at[1])
    load_screen = pltpu.make_async_copy(
        screen_hbm.at[pl.ds(0, half)], screen_ref, sems.at[2]
    )
    load_old.start()
    load_table.start()
    load_screen.start()
    acc_ref[...] = jnp.zeros_like(acc_ref)
    load_back.wait()
    add_blocks(
        row_ref, got_ref, phase_ref, expand_ref, back_ref, coeff_ref, acc_ref, size
    )
    load_old.wait()

    def first_step(i, carry):
        at = pl.multiple_of(i * 16, 16)
        for half in range(2):
            x = [
                tuple(
                    acc_ref[2 * p + half, pl.ds(at + U0 * k, 16), :]
                    + old_ref[2 * p + half, pl.ds(at + U0 * k, 16), :]
                    for p in range(2)
                )
                for k in range(U1)
            ]
            even = dft8(x)
            for k in range(1, U1):
                c, s = math.cos(math.pi * k / U1), math.sin(math.pi * k / U1)
                x[k] = (x[k][0] * c - x[k][1] * s, x[k][0] * s + x[k][1] * c)
            for ref, out in ((mid_ref, even), (odd_ref, dft8(x))):
                for k in range(L0 // 2):
                    for p in range(2):
                        ref[k, pl.ds(U0 * p + at, 16), half * 128 : (half + 1) * 128] = out[k][
                            p
                        ].astype(jnp.bfloat16)
        return carry

    lax.fori_loop(0, U0 // 16, first_step, 0, unroll=2)
    load_table.wait()
    load_screen.wait()
    finish(place_ref, [table_ref], mid_ref, screen_ref, full_ref, keep_ref, send_ref)


def odd_kernel(place_ref, mid_ref, screen_ref, *refs):
    *table_refs, keep_ref, send_ref, full_ref = refs
    finish(place_ref, table_refs, mid_ref, screen_ref, full_ref, keep_ref, send_ref)


def make_image(
    rows, place, got, phase, expand, back_shape, old, tables, screens, size
):
    vmem = pl.BlockSpec(memory_space=pltpu.VMEM)
    smem = pl.BlockSpec(memory_space=pltpu.SMEM)
    hbm = pl.BlockSpec(memory_space=pl.ANY)
    half = L0 // 2
    piece = jax.ShapeDtypeStruct((place.shape[1], half, 16, COLS), jnp.bfloat16)
    mid = (half, 2 * U0, COLS)
    buffers = [
        pltpu.VMEM((half, *tables[0].shape[1:]), jnp.bfloat16),
        pltpu.VMEM(screens[1].shape, jnp.bfloat16),
        pltpu.VMEM((16, half, 16, COLS), jnp.bfloat16),
    ]
    keep, send, odd = pl.pallas_call(
        functools.partial(even_kernel, size=size),
        out_shape=(piece, piece, jax.ShapeDtypeStruct(mid, jnp.bfloat16)),
        in_specs=[smem, smem, vmem, vmem, vmem, hbm, hbm, hbm],
        out_specs=(vmem, vmem, vmem),
        scratch_shapes=[
            pltpu.VMEM(back_shape, jnp.bfloat16),
            coeff_scratch(got, size),
            pltpu.VMEM(old.shape, jnp.float32),
            pltpu.VMEM(old.shape, jnp.float32),
            buffers[0],
            pltpu.VMEM(mid, jnp.bfloat16),
            *buffers[1:],
            pltpu.SemaphoreType.DMA((4,)),
        ],
        compiler_params=pltpu.CompilerParams(vmem_limit_bytes=EVEN_MIB * MIB),
        cost_estimate=pl.CostEstimate(
            flops=16 * 1024**3, bytes_accessed=24 * MIB, transcendentals=0
        ),
    )(rows, place, got, phase, expand, old, tables[0], screens[0])
    keep_odd, send_odd = pl.pallas_call(
        odd_kernel,
        out_shape=(piece, piece),
        in_specs=[smem, *[vmem] * (2 + len(tables[1]))],
        out_specs=(vmem, vmem),
        scratch_shapes=[buffers[2]],
        compiler_params=pltpu.CompilerParams(vmem_limit_bytes=ODD_MIB * MIB),
        cost_estimate=pl.CostEstimate(
            flops=4 * 1024**3, bytes_accessed=12 * MIB, transcendentals=0
        ),
    )(place, odd, screens[1], *tables[1])
    return (keep, send), (keep_odd, send_odd)


def screen_kernel(base_ref, w_ref, even_ref, odd_ref, *, scale):
    cell = 2.0 * FIELD / N
    col = base_ref[0] + lax.broadcasted_iota(jnp.int32, (1, COLS), 1)
    dm = col.astype(jnp.float32) * cell
    for half, out_ref in enumerate((even_ref, odd_ref)):
        l0 = 2 * pl.program_id(0) + half
        row = l0 + L0 * lax.broadcasted_iota(jnp.int32, (L1, 1), 0)
        dl = row.astype(jnp.float32) * cell
        lift = jnp.sqrt((1.0 - dl * dl) - dm * dm) - 1.0
        quarters = (4.0 * w_ref[0]) * lift
        c, s = turned(quarters, row + col, scale)
        out_ref[0, 0] = c.astype(out_ref.dtype)
        out_ref[0, 1] = s.astype(out_ref.dtype)


def make_screen(base, w, scale):
    smem = pl.BlockSpec(memory_space=pltpu.SMEM)
    half = jax.ShapeDtypeStruct((L0 // 2, 2, L1, COLS), jnp.bfloat16)
    wide = jax.ShapeDtypeStruct((2 * L0, 2, L1, COLS), jnp.bfloat16)
    spec = pl.BlockSpec((1, 2, L1, COLS), lambda k: (k, 0, 0, 0))
    return pl.pallas_call(
        functools.partial(screen_kernel, scale=scale),
        out_shape=(wide, half),
        grid=(L0 // 2,),
        in_specs=[smem, smem],
        out_specs=(spec, spec),
        compiler_params=pltpu.CompilerParams(vmem_limit_bytes=60 * MIB),
        cost_estimate=pl.CostEstimate(
            flops=40 * HALF * COLS, bytes_accessed=8 * MIB, transcendentals=HALF * COLS
        ),
    )(base, w)


def sum_planes(keep, send, planes):
    def shifted(values, target):
        pairs = [(i, target(i)) for i in range(planes)]
        return lax.ppermute(values, "wa", pairs).astype(jnp.float32)

    total = keep.astype(jnp.float32) + shifted(send, lambda i: i ^ 1)
    total = total.astype(jnp.bfloat16).reshape(4, 2, L0 // 2, 16, COLS)
    got = [
        shifted(total[step], lambda i, step=step: (i + 4 * step) % planes) for step in (1, 2, 3)
    ]
    total = (total[0].astype(jnp.float32) + got[0] + got[1] + got[2]).astype(jnp.bfloat16)
    return total[0].astype(jnp.float32) + shifted(total[1], lambda i: i ^ 2)


def body(kernel_u, kernel_v, visibilities, vis_count, tile_route, block_offset, plane_w):
    n_tu, n_tv, planes = lax.axis_size("tu"), lax.axis_size("tv"), lax.axis_size("wa")
    owners = n_tu * n_tv
    blocks, slots = kernel_u.shape[0], kernel_u.shape[1]
    size = blocks // CHUNKS
    project, expand = factor_tables(n_tu, n_tv)
    tables = row_tables()
    keep, back = keep_tables(size)
    slab = np.zeros((1, *tables[0].shape[1:]), tables[0].dtype)
    slab[0, : back.shape[0], : back.shape[1]] = back
    tables = (np.concatenate([tables[0], slab]), tables[1])

    owner = lax.axis_index(("tu", "tv"))
    col_base = owner * COLS
    scale = 1.0 / math.sqrt(slots * blocks * owners * 16)
    screens = make_screen(col_base.reshape(1), plane_w, scale)
    got = []
    for chunk in range(CHUNKS):
        coeffs = project_chunk(
            vis_count, tile_route.T, block_offset.T, kernel_u, kernel_v, visibilities, project, keep,
            owners, n_tv, chunk, size,
        )
        if chunk:
            coeffs, screens = lax.optimization_barrier((coeffs, screens))
        got.append(
            lax.all_to_all(coeffs, ("tv", "tu"), split_axis=0, concat_axis=0, tiled=True)
        )
    marks = got[0][:, MARK, : 4 * blocks].astype(jnp.int32).reshape(owners, 2, 2, blocks)
    corners = marks[:, :, 0] * 64 + marks[:, :, 1]
    first = (corners[:, 1] * col_base + N // 4 * corners[:, 0]) % N
    rows, phase = [], []
    for chunk in range(CHUNKS):
        mine = slice(chunk * size, (chunk + 1) * size)
        rows.append(corners[:, 0, mine].reshape(-1))
        phase.append(jnp.stack([corners[:, 1, mine], first[:, mine]], axis=2).reshape(-1, 2))

    me = lax.axis_index("wa")
    core, z_hi, x = me % 2, me // 2 % 2, me // 4
    step = jnp.arange(8, dtype=jnp.int32)
    pair = ((x + step // 2) % 4) * 4 + (z_hi ^ (step % 2)) * 2
    place = jnp.stack([pair + core, pair + (1 - core)])

    acc = grid_chunk(rows[0], got[0], phase[0], expand, back, size)
    halves = make_image(
        rows[1], place, got[1], phase[1], expand, back.shape, acc, tables, screens, size
    )
    if planes != 16:
        return halves
    even, odd = (sum_planes(keep, send, planes) for keep, send in halves)
    return jnp.stack([even, odd], axis=1).transpose(2, 0, 1, 3).reshape(L0 * 16, COLS)


def solution(mesh):
    split = ("wa", "tu", "tv")
    placed = (
        P(split, None, None),
        P(split, None, None),
        P(split, None, None),
        P(split),
        P(split, None),
        P(split, None),
        P("wa"),
    )
    return jax.shard_map(
        body, mesh=mesh, in_specs=placed, out_specs=P("wa", ("tu", "tv")), check_vma=False
    )
```

```python
import functools
import math

import jax
import jax.numpy as jnp
import ml_dtypes
import numpy as np
from jax import lax
from jax.experimental import pallas as pl
from jax.experimental.pallas import tpu as pltpu
from jax.sharding import PartitionSpec as P

N = 8192
HALF = 4096
S = 128
RANK = 14
ROWS = 2 * RANK
STACK = 32
PACKED = 144
MARK = 140
KEPT = 80
PIECE = 1
COLS = 256
U0 = 512
U1 = 8
L0 = 16
L1 = 256
TILE = 1024
CHUNKS = 2
FIELD = 0.25
MIB = 1 << 20
EVEN_MIB = 45
ODD_MIB = 22


def prolate(count, half_band):
    n = np.arange(S)
    diagonal = ((S - 1 - 2 * n) / 2) ** 2 * np.cos(2 * np.pi * half_band)
    beside = n[1:] * (S - n[1:]) / 2
    _, v = np.linalg.eigh(np.diag(diagonal) + np.diag(beside, 1) + np.diag(beside, -1))
    v = v[:, ::-1][:, :count]
    peak = np.argmax(np.abs(v[: S // 2]), axis=0)
    return v * np.sign(v[peak, np.arange(count)])


def factor_tables(n_tu, n_tv):
    t = np.arange(S) - (S - 1) / 2
    mu = np.arange(COLS) - (COLS - 1) / 2
    basis = prolate(RANK, COLS / 2 / N)
    spread = basis.T @ np.exp(2j * np.pi * np.outer(t, mu) / N)
    project = []
    for pad in ((0, STACK - ROWS), (STACK - ROWS, 0)):
        rows = []
        for j in [tu * n_tv + tv for tv in range(n_tv) for tu in range(n_tu)]:
            centre = COLS * j + (COLS - 1) / 2
            turn = np.exp(2j * np.pi * np.arange(S) * centre / N)
            proj = basis.T * turn[None, :]
            rows.append(np.pad(np.block([[proj.real, -proj.imag], [proj.imag, proj.real]]), (pad, (0, 0))))
        project.append(np.concatenate(rows, axis=0))
    sr, si = spread.real, spread.imag
    pad = ((0, STACK - ROWS), (0, 0))
    by_cos = np.pad(np.block([[sr, si], [-si, sr]]), pad).astype(np.float32)
    by_sin = np.pad(np.block([[-si, sr], [-sr, -si]]), pad).astype(np.float32)
    return np.stack(project).astype(ml_dtypes.bfloat16), np.stack([by_cos, by_sin])


def keep_spans(size):
    width = size * KEPT
    runs = [(lo, min(lo + 256, width)) for lo in range(0, width, 256)]
    return [(lo, hi, lo // KEPT, -(-hi // KEPT)) for lo, hi in runs]


def keep_tables(size):
    whole = np.kron(np.eye(size), prolate(KEPT, 0.25)).astype(ml_dtypes.bfloat16)
    to = [
        np.pad(whole[b0 * S : b1 * S, lo:hi], ((0, 0), (0, 256 - (hi - lo))))
        for lo, hi, b0, b1 in keep_spans(size)
    ]
    back = []
    for g in range(size // 2):
        lo = 2 * KEPT * g // 128 * 128
        back.append(whole[2 * S * g : 2 * S * (g + 1), lo : lo + 256].T)
    return np.concatenate(to, axis=0), np.concatenate(back, axis=1)


def row_tables():
    u0 = np.arange(U0)[None, None, :]
    l0 = np.arange(L0)[:, None, None]
    l1 = np.arange(L1)[None, :, None]
    a = 2.0 * np.pi * ((u0 * (l0 + L0 * l1 - N // 4)) % N) / N
    c, s = np.cos(a).astype(ml_dtypes.bfloat16), np.sin(a).astype(ml_dtypes.bfloat16)
    table = np.concatenate(
        [np.concatenate([c, -s], axis=2), np.concatenate([s, c], axis=2)], axis=1
    )
    return table[0::2], [table[k : 2 * PIECE + k : 2] for k in range(1, L0, 2 * PIECE)]


def turned(quarters, back, scale):
    h = math.pi / 2
    whole = jnp.floor(quarters + 0.5)
    f = quarters - whole
    count = whole.astype(jnp.int32) - back
    t = f * f
    sine, cosine = 0.0, 0.0
    for n in (9, 7, 5, 3, 1):
        sine = sine * t + (-1) ** (n // 2) * h**n / math.factorial(n) * scale
    for n in (10, 8, 6, 4, 2, 0):
        cosine = cosine * t + (-1) ** (n // 2) * h**n / math.factorial(n) * scale
    sine = sine * f
    odd = (count & 1) == 1
    c = jnp.where(odd, sine, cosine)
    s = jnp.where(odd, cosine, sine)
    return (
        jnp.where(((count + 1) & 2) == 2, -c, c),
        jnp.where((count & 2) == 2, -s, s),
    )


def corner_marks(route_ref, offset_ref, n_tv):
    lane = lax.broadcasted_iota(jnp.int32, (1, S), 1)
    marks = jnp.zeros((1, S), jnp.int32)
    blocks = route_ref.shape[1]
    for b in range(blocks):
        tile = route_ref[0, b]
        place = (tile // n_tv, tile % n_tv)
        for axis in range(2):
            corner = place[axis] * TILE + offset_ref[axis, b]
            at = 2 * blocks * axis + b
            marks = jnp.where(lane == at, corner // 64, marks)
            marks = jnp.where(lane == at + blocks, corner % 64, marks)
    return marks.astype(jnp.float32)


def project_kernel(
    count_ref, route_ref, offset_ref, ku_ref, kv_ref, vis_ref, table_ref, keep_ref, out_ref,
    *, first, n_tv,
):
    slots = lax.broadcasted_iota(jnp.int32, (2, ku_ref.shape[1]), 1)
    owners, rows, _ = out_ref.shape
    turn = lax.broadcasted_iota(jnp.int32, (1, S), 1) & 3
    cosine = jnp.where(turn == 0, 1.0, jnp.where(turn == 2, -1.0, 0.0))
    sine = jnp.where(turn == 1, 1.0, jnp.where(turn == 3, -1.0, 0.0))
    subs = []
    for b in range(ku_ref.shape[0]):
        live = count_ref[first + b]
        vis = jnp.where(slots < live, vis_ref[b].astype(jnp.float32), 0.0)
        kv_t = kv_ref[b].astype(jnp.float32).T
        weighted = jnp.concatenate([kv_t * vis[0:1, :], kv_t * vis[1:2, :]], axis=0)
        sub = jnp.dot(
            weighted.astype(jnp.bfloat16), ku_ref[b], preferred_element_type=jnp.float32
        )
        re, im = sub[:S], sub[S:]
        subs.append(
            jnp.concatenate(
                [re * cosine - im * sine, re * sine + im * cosine], axis=0
            ).astype(jnp.bfloat16)
        )
    start, runs = 0, []
    for lo, hi, b0, b1 in keep_spans(ku_ref.shape[0]):
        depth = (b1 - b0) * S
        kept = jnp.dot(
            jnp.concatenate(subs[b0:b1], axis=1),
            keep_ref[start : start + depth, : hi - lo],
            preferred_element_type=jnp.float32,
        ).astype(jnp.bfloat16)
        start += depth
        runs += [kept[:, i : i + 128] for i in range(0, hi - lo, 128)]

    tiles = [None] * len(runs)
    for which in range(2):
        mine = list(range(which, len(runs), 2))
        for i in range(0, len(mine), 2):
            pair = mine[i : i + 2]
            out = jnp.dot(
                table_ref[which],
                jnp.concatenate([runs[t] for t in pair], axis=1),
                preferred_element_type=jnp.float32,
            ).reshape(owners, STACK, 128 * len(pair))
            for n, t in enumerate(pair):
                tiles[t] = out[:, :, 128 * n : 128 * (n + 1)]
    whole, part = ROWS // 8 * 8, STACK - ROWS
    pieces = []
    for t in range(0, len(tiles), 2):
        pieces.append(tiles[t][:, :whole])
        if t + 1 < len(tiles):
            pieces += [tiles[t][:, whole:] + tiles[t + 1][:, :8], tiles[t + 1][:, 8:]]
        else:
            line = lax.broadcasted_iota(jnp.int32, (8, S), 0)
            marks = corner_marks(route_ref, offset_ref, n_tv) if first == 0 else 0.0
            last = jnp.where((line == MARK % 8)[None], marks, tiles[t][:, whole:])
            pieces += [last, jnp.zeros((owners, rows - MARK // 8 * 8 - 8, S), jnp.float32)]
    pieces = [p for p in pieces if p.shape[1]]
    out_ref[...] = jnp.concatenate(pieces, axis=1).astype(jnp.bfloat16)


def project_chunk(count, route, offset, ku, kv, vis, table, keep, owners, n_tv, chunk, size):
    slots = ku.shape[1]
    return pl.pallas_call(
        functools.partial(project_kernel, first=chunk * size, n_tv=n_tv),
        out_shape=jax.ShapeDtypeStruct((owners, PACKED, S), jnp.bfloat16),
        grid_spec=pltpu.PrefetchScalarGridSpec(
            num_scalar_prefetch=3,
            grid=(1,),
            in_specs=[
                pl.BlockSpec((size, slots, S), lambda b, *_: (chunk, 0, 0)),
                pl.BlockSpec((size, slots, S), lambda b, *_: (chunk, 0, 0)),
                pl.BlockSpec((size, 2, slots), lambda b, *_: (chunk, 0, 0)),
                pl.BlockSpec(table.shape, lambda b, *_: (0, 0, 0)),
                pl.BlockSpec(keep.shape, lambda b, *_: (0, 0)),
            ],
            out_specs=pl.BlockSpec((owners, PACKED, S), lambda b, *_: (0, 0, 0)),
        ),
        compiler_params=pltpu.CompilerParams(vmem_limit_bytes=60 * MIB),
        cost_estimate=pl.CostEstimate(
            flops=size * 2 * (256 * 256 * 128 + 512 * 256 * 128),
            bytes_accessed=size * 4 * 65536,
            transcendentals=0,
        ),
    )(count, route, offset, ku, kv, vis, table, keep)


def add_blocks(
    row_ref, got_ref, phase_ref, expand_ref, back_ref, coeff_ref, acc_ref, size
):
    sources = got_ref.shape[0]
    packed = got_ref[...].astype(jnp.float32)
    blank = jnp.zeros((sources, STACK - ROWS, S), jnp.float32)
    tiles = [
        jnp.concatenate([packed[:, ROWS * t : ROWS * (t + 1)], blank], axis=1)
        .astype(jnp.bfloat16)
        .reshape(sources * STACK, S)
        for t in range(size * KEPT // S)
    ]
    for g in range(size // 2):
        t = 2 * KEPT * g // S
        part = jnp.dot(
            jnp.concatenate(tiles[t : t + 2], axis=1),
            back_ref[:, 256 * g : 256 * (g + 1)],
            preferred_element_type=jnp.float32,
        )
        coeff_ref[:, :, 256 * g : 256 * (g + 1)] = part.astype(jnp.bfloat16).reshape(
            sources, STACK, 256
        )
    by_cos, by_sin = expand_ref[0], expand_ref[1]

    lane = lax.broadcasted_iota(jnp.int32, (1, COLS), 1)
    centre = (S - 1) / 2 * (lane.astype(jnp.float32) - (COLS - 1) / 2)

    def per_source(src, carry):
        base = phase_ref[pl.ds(pl.multiple_of(src * size, size), size), :]
        turns = (base[:, 0:1] * lane + base[:, 1:2]) & (N - 1)
        phases = jnp.concatenate(
            turned((turns.astype(jnp.float32) + centre) * (4.0 / N), 0, 1.0), axis=1
        )
        for b in range(size):
            row = row_ref[src * size + b]
            ph = phases[b : b + 1]
            c = jnp.concatenate([ph[:, :COLS], ph[:, :COLS]], axis=1)
            s = jnp.concatenate([ph[:, COLS:], ph[:, COLS:]], axis=1)
            weights = (by_cos * c + by_sin * s).astype(jnp.bfloat16)
            coeffs = coeff_ref[src, :, b * S : (b + 1) * S]
            block = lax.dot_general(
                coeffs, weights, (((0,), (0,)), ((), ())), preferred_element_type=jnp.float32
            )
            for q in range(4):
                acc_ref[q, pl.ds(row, S), :] += block[:, q * 128 : (q + 1) * 128]
        return carry

    lax.fori_loop(0, sources, per_source, 0, unroll=8)


def grid_kernel(
    row_ref, got_ref, phase_ref, expand_ref, back_ref, out_ref, coeff_ref, *, size
):
    out_ref[...] = jnp.zeros_like(out_ref)
    add_blocks(
        row_ref, got_ref, phase_ref, expand_ref, back_ref, coeff_ref, out_ref, size
    )


def coeff_scratch(got, size):
    return pltpu.VMEM((got.shape[0], STACK, size * S), jnp.bfloat16)


def grid_chunk(rows, got, phase, expand, back, size):
    vmem = pl.BlockSpec(memory_space=pltpu.VMEM)
    return pl.pallas_call(
        functools.partial(grid_kernel, size=size),
        out_shape=jax.ShapeDtypeStruct((4, HALF, 128), jnp.float32),
        in_specs=[pl.BlockSpec(memory_space=pltpu.SMEM), vmem, vmem, vmem, vmem],
        out_specs=vmem,
        scratch_shapes=[coeff_scratch(got, size)],
        compiler_params=pltpu.CompilerParams(vmem_limit_bytes=56 * MIB),
        cost_estimate=pl.CostEstimate(
            flops=got.shape[0] * size * 2 * 128 * 256 * 512,
            bytes_accessed=12 * MIB,
            transcendentals=0,
        ),
    )(rows, got, phase, expand, back)


def dft8(x):
    def add(p, q):
        return (p[0] + q[0], p[1] + q[1])

    def sub(p, q):
        return (p[0] - q[0], p[1] - q[1])

    def turn(p):
        return (-p[1], p[0])

    def dft4(a, b, c, d):
        s, t, v, w = add(a, c), sub(a, c), add(b, d), turn(sub(b, d))
        return add(s, v), add(t, w), sub(s, v), sub(t, w)

    h = math.sqrt(0.5)
    e = dft4(x[0], x[2], x[4], x[6])
    o = list(dft4(x[1], x[3], x[5], x[7]))
    o[1] = ((o[1][0] - o[1][1]) * h, (o[1][0] + o[1][1]) * h)
    o[2] = turn(o[2])
    o[3] = ((-o[3][0] - o[3][1]) * h, (o[3][0] - o[3][1]) * h)
    return [add(e[k], o[k]) for k in range(4)] + [sub(e[k], o[k]) for k in range(4)]


def finish(place_ref, table_refs, mid_ref, screen_ref, full_ref, keep_ref, send_ref):
    for k in range(L0 // 2):
        ref = table_refs[k // table_refs[0].shape[0]]
        planar = jnp.dot(
            ref[k % ref.shape[0]], mid_ref[k], preferred_element_type=jnp.float32
        )
        c, s = (screen_ref[k, p].astype(jnp.float32) for p in range(2))
        value = planar[:L1] * c - planar[L1:] * s
        full_ref[:, k] = value.astype(jnp.bfloat16).reshape(L1 // 16, 16, COLS)
    for out_ref, which in ((keep_ref, 0), (send_ref, 1)):
        for i in range(out_ref.shape[0]):
            out_ref[i] = full_ref[place_ref[which, i]]


def even_kernel(
    row_ref, place_ref, got_ref, phase_ref, expand_ref, old_hbm, table_hbm, screen_hbm,
    keep_ref, send_ref, odd_ref,
    back_ref, coeff_ref, acc_ref, old_ref, table_ref, mid_ref, screen_ref, full_ref, sems,
    *, size,
):
    load_old = pltpu.make_async_copy(old_hbm, old_ref, sems.at[0])
    half = L0 // 2
    load_back = pltpu.make_async_copy(
        table_hbm.at[half, pl.ds(0, back_ref.shape[0])], back_ref, sems.at[3]
    )
    load_back.start()
    load_table = pltpu.make_async_copy(table_hbm.at[pl.ds(0, half)], table_ref, sems.at[1])
    load_screen = pltpu.make_async_copy(
        screen_hbm.at[pl.ds(0, half)], screen_ref, sems.at[2]
    )
    load_old.start()
    load_table.start()
    load_screen.start()
    acc_ref[...] = jnp.zeros_like(acc_ref)
    load_back.wait()
    add_blocks(
        row_ref, got_ref, phase_ref, expand_ref, back_ref, coeff_ref, acc_ref, size
    )
    load_old.wait()

    def first_step(i, carry):
        at = pl.multiple_of(i * 16, 16)
        for half in range(2):
            x = [
                tuple(
                    acc_ref[2 * p + half, pl.ds(at + U0 * k, 16), :]
                    + old_ref[2 * p + half, pl.ds(at + U0 * k, 16), :]
                    for p in range(2)
                )
                for k in range(U1)
            ]
            even = dft8(x)
            for k in range(1, U1):
                c, s = math.cos(math.pi * k / U1), math.sin(math.pi * k / U1)
                x[k] = (x[k][0] * c - x[k][1] * s, x[k][0] * s + x[k][1] * c)
            for ref, out in ((mid_ref, even), (odd_ref, dft8(x))):
                for k in range(L0 // 2):
                    for p in range(2):
                        ref[k, pl.ds(U0 * p + at, 16), half * 128 : (half + 1) * 128] = out[k][
                            p
                        ].astype(jnp.bfloat16)
        return carry

    lax.fori_loop(0, U0 // 16, first_step, 0, unroll=4)
    load_table.wait()
    load_screen.wait()
    finish(place_ref, [table_ref], mid_ref, screen_ref, full_ref, keep_ref, send_ref)


def odd_kernel(place_ref, mid_ref, screen_ref, *refs):
    *table_refs, keep_ref, send_ref, full_ref = refs
    finish(place_ref, table_refs, mid_ref, screen_ref, full_ref, keep_ref, send_ref)


def make_image(
    rows, place, got, phase, expand, back_shape, old, tables, screens, size
):
    vmem = pl.BlockSpec(memory_space=pltpu.VMEM)
    smem = pl.BlockSpec(memory_space=pltpu.SMEM)
    hbm = pl.BlockSpec(memory_space=pl.ANY)
    half = L0 // 2
    piece = jax.ShapeDtypeStruct((place.shape[1], half, 16, COLS), jnp.bfloat16)
    mid = (half, 2 * U0, COLS)
    buffers = [
        pltpu.VMEM((half, *tables[0].shape[1:]), jnp.bfloat16),
        pltpu.VMEM(screens[1].shape, jnp.bfloat16),
        pltpu.VMEM((16, half, 16, COLS), jnp.bfloat16),
    ]
    keep, send, odd = pl.pallas_call(
        functools.partial(even_kernel, size=size),
        out_shape=(piece, piece, jax.ShapeDtypeStruct(mid, jnp.bfloat16)),
        in_specs=[smem, smem, vmem, vmem, vmem, hbm, hbm, hbm],
        out_specs=(vmem, vmem, vmem),
        scratch_shapes=[
            pltpu.VMEM(back_shape, jnp.bfloat16),
            coeff_scratch(got, size),
            pltpu.VMEM(old.shape, jnp.float32),
            pltpu.VMEM(old.shape, jnp.float32),
            buffers[0],
            pltpu.VMEM(mid, jnp.bfloat16),
            *buffers[1:],
            pltpu.SemaphoreType.DMA((4,)),
        ],
        compiler_params=pltpu.CompilerParams(vmem_limit_bytes=EVEN_MIB * MIB),
        cost_estimate=pl.CostEstimate(
            flops=16 * 1024**3, bytes_accessed=24 * MIB, transcendentals=0
        ),
    )(rows, place, got, phase, expand, old, tables[0], screens[0])
    keep_odd, send_odd = pl.pallas_call(
        odd_kernel,
        out_shape=(piece, piece),
        in_specs=[smem, *[vmem] * (2 + len(tables[1]))],
        out_specs=(vmem, vmem),
        scratch_shapes=[buffers[2]],
        compiler_params=pltpu.CompilerParams(vmem_limit_bytes=ODD_MIB * MIB),
        cost_estimate=pl.CostEstimate(
            flops=4 * 1024**3, bytes_accessed=12 * MIB, transcendentals=0
        ),
    )(place, odd, screens[1], *tables[1])
    return (keep, send), (keep_odd, send_odd)


def screen_kernel(base_ref, w_ref, even_ref, odd_ref, *, scale):
    cell = 2.0 * FIELD / N
    col = base_ref[0] + lax.broadcasted_iota(jnp.int32, (1, COLS), 1)
    dm = col.astype(jnp.float32) * cell
    for half, out_ref in enumerate((even_ref, odd_ref)):
        l0 = 2 * pl.program_id(0) + half
        row = l0 + L0 * lax.broadcasted_iota(jnp.int32, (L1, 1), 0)
        dl = row.astype(jnp.float32) * cell
        lift = jnp.sqrt((1.0 - dl * dl) - dm * dm) - 1.0
        quarters = (4.0 * w_ref[0]) * lift
        c, s = turned(quarters, row + col, scale)
        out_ref[0, 0] = c.astype(out_ref.dtype)
        out_ref[0, 1] = s.astype(out_ref.dtype)


def make_screen(base, w, scale):
    smem = pl.BlockSpec(memory_space=pltpu.SMEM)
    half = jax.ShapeDtypeStruct((L0 // 2, 2, L1, COLS), jnp.bfloat16)
    wide = jax.ShapeDtypeStruct((2 * L0, 2, L1, COLS), jnp.bfloat16)
    spec = pl.BlockSpec((1, 2, L1, COLS), lambda k: (k, 0, 0, 0))
    return pl.pallas_call(
        functools.partial(screen_kernel, scale=scale),
        out_shape=(wide, half),
        grid=(L0 // 2,),
        in_specs=[smem, smem],
        out_specs=(spec, spec),
        compiler_params=pltpu.CompilerParams(vmem_limit_bytes=60 * MIB),
        cost_estimate=pl.CostEstimate(
            flops=40 * HALF * COLS, bytes_accessed=8 * MIB, transcendentals=HALF * COLS
        ),
    )(base, w)


def sum_planes(keep, send, planes):
    def shifted(values, target):
        pairs = [(i, target(i)) for i in range(planes)]
        return lax.ppermute(values, "wa", pairs).astype(jnp.float32)

    total = keep.astype(jnp.float32) + shifted(send, lambda i: i ^ 1)
    total = total.astype(jnp.bfloat16).reshape(4, 2, L0 // 2, 16, COLS)
    got = [
        shifted(total[step], lambda i, step=step: (i + 4 * step) % planes) for step in (1, 2, 3)
    ]
    total = (total[0].astype(jnp.float32) + got[0] + got[1] + got[2]).astype(jnp.bfloat16)
    return total, lax.ppermute(total[1], "wa", [(i, i ^ 2) for i in range(planes)])


def last_kernel(even_ref, even_got_ref, odd_ref, odd_got_ref, out_ref, rows_ref):
    for half, (ref, got_ref) in enumerate(((even_ref, even_got_ref), (odd_ref, odd_got_ref))):
        for k in range(L0 // 2):
            value = ref[0, k].astype(jnp.float32) + got_ref[k].astype(jnp.float32)
            for c in range(2):
                rows_ref[c, pl.ds(2 * k + half, 16, stride=L0), :] = value[
                    :, 128 * c : 128 * (c + 1)
                ]
    for c in range(2):
        out_ref[:, 128 * c : 128 * (c + 1)] = rows_ref[c]


def last_sum(even, odd):
    vmem = pl.BlockSpec(memory_space=pltpu.VMEM)
    return pl.pallas_call(
        last_kernel,
        out_shape=jax.ShapeDtypeStruct((L0 * 16, COLS), jnp.float32),
        in_specs=[vmem] * 4,
        out_specs=vmem,
        scratch_shapes=[pltpu.VMEM((2, L0 * 16, 128), jnp.float32)],
        compiler_params=pltpu.CompilerParams(vmem_limit_bytes=16 * MIB),
        cost_estimate=pl.CostEstimate(
            flops=10**8, bytes_accessed=MIB, transcendentals=0
        ),
    )(*even, *odd)


def body(kernel_u, kernel_v, visibilities, vis_count, tile_route, block_offset, plane_w):
    n_tu, n_tv, planes = lax.axis_size("tu"), lax.axis_size("tv"), lax.axis_size("wa")
    owners = n_tu * n_tv
    blocks, slots = kernel_u.shape[0], kernel_u.shape[1]
    size = blocks // CHUNKS
    project, expand = factor_tables(n_tu, n_tv)
    tables = row_tables()
    keep, back = keep_tables(size)
    slab = np.zeros((1, *tables[0].shape[1:]), tables[0].dtype)
    slab[0, : back.shape[0], : back.shape[1]] = back
    tables = (np.concatenate([tables[0], slab]), tables[1])

    owner = lax.axis_index(("tu", "tv"))
    col_base = owner * COLS
    scale = 1.0 / math.sqrt(slots * blocks * owners * 16)
    screens = make_screen(col_base.reshape(1), plane_w, scale)
    got = []
    for chunk in range(CHUNKS):
        coeffs = project_chunk(
            vis_count, tile_route.T, block_offset.T, kernel_u, kernel_v, visibilities, project, keep,
            owners, n_tv, chunk, size,
        )
        if chunk:
            coeffs, screens = lax.optimization_barrier((coeffs, screens))
        got.append(
            lax.all_to_all(coeffs, ("tv", "tu"), split_axis=0, concat_axis=0, tiled=True)
        )
    marks = got[0][:, MARK, : 4 * blocks].astype(jnp.int32).reshape(owners, 2, 2, blocks)
    corners = marks[:, :, 0] * 64 + marks[:, :, 1]
    first = (corners[:, 1] * col_base + N // 4 * corners[:, 0]) % N
    rows, phase = [], []
    for chunk in range(CHUNKS):
        mine = slice(chunk * size, (chunk + 1) * size)
        rows.append(corners[:, 0, mine].reshape(-1))
        phase.append(jnp.stack([corners[:, 1, mine], first[:, mine]], axis=2).reshape(-1, 2))

    me = lax.axis_index("wa")
    core, z_hi, x = me % 2, me // 2 % 2, me // 4
    step = jnp.arange(8, dtype=jnp.int32)
    pair = ((x + step // 2) % 4) * 4 + (z_hi ^ (step % 2)) * 2
    place = jnp.stack([pair + core, pair + (1 - core)])

    acc = grid_chunk(rows[0], got[0], phase[0], expand, back, size)
    halves = make_image(
        rows[1], place, got[1], phase[1], expand, back.shape, acc, tables, screens, size
    )
    if planes != 16:
        return halves
    even, odd = (sum_planes(keep, send, planes) for keep, send in halves)
    return last_sum(even, odd)


def solution(mesh):
    split = ("wa", "tu", "tv")
    placed = (
        P(split, None, None),
        P(split, None, None),
        P(split, None, None),
        P(split),
        P(split, None),
        P(split, None),
        P("wa"),
    )
    return jax.shard_map(
        body, mesh=mesh, in_specs=placed, out_specs=P("wa", ("tu", "tv")), check_vma=False
    )
```
